32 devices in a mesh: dp: 32 (over z, y, x, core).
Axes of the slice: x: 2, y: 2, z: 4, core: 2. Of those that a mesh axis runs over, the one named last changes fastest.
Arguments:
- tokens: bfloat16 [4096, 768], P('dp'), may hold values from -6 to 6
- lengths: int32 [64], P('dp'), may hold values from 0 to 128, as said below
- qkv_weight: bfloat16 [768, 2304], P('dp'), may hold values from -0.21875 to 0.21875
- query_bias: bfloat16 [768], P('dp'), may hold values from -3 to 3
- value_bias: bfloat16 [768], P('dp'), may hold values from -3 to 3
- out_weight: bfloat16 [768, 768], P('dp'), may hold values from -0.875 to 0.875
- out_bias: bfloat16 [768], P('dp'), may hold values from -3 to 3
- norm_one_gain: bfloat16 [768], P('dp'), may hold values from 0.5 to 1.5
- norm_one_shift: bfloat16 [768], P('dp'), may hold values from -3 to 3
- ff_in_weight: bfloat16 [768, 3072], P('dp'), may hold values from -0.21875 to 0.21875
- ff_in_bias: bfloat16 [3072], P('dp'), may hold values from -3 to 3
- ff_out_weight: bfloat16 [3072, 768], P('dp'), may hold values from -0.109375 to 0.109375
- ff_out_bias: bfloat16 [768], P('dp'), may hold values from -3 to 3
- norm_two_gain: bfloat16 [768], P('dp'), may hold values from 0.5 to 1.5
- norm_two_shift: bfloat16 [768], P('dp'), may hold values from -3 to 3
- out_grad: bfloat16 [4096, 768], P('dp'), may hold values from -6 to 6
Outputs:
- encoded: bfloat16 [4096, 768], P('dp')
- grad_tokens: float32 [4096, 768], P('dp')
- grad_qkv_weight: float32 [768, 2304], P('dp')
- grad_query_bias: float32 [768], P('dp')
- grad_value_bias: float32 [768], P('dp')
- grad_out_weight: float32 [768, 768], P('dp')
- grad_out_bias: float32 [768], P('dp')
- grad_norm_one_gain: float32 [768], P('dp')
- grad_norm_one_shift: float32 [768], P('dp')
- grad_ff_in_weight: float32 [768, 3072], P('dp')
- grad_ff_in_bias: float32 [3072], P('dp')
- grad_ff_out_weight: float32 [3072, 768], P('dp')
- grad_ff_out_bias: float32 [768], P('dp')
- grad_norm_two_gain: float32 [768], P('dp')
- grad_norm_two_shift: float32 [768], P('dp')
The draws below stay inside these ranges and needn't reach their ends.
Inputs may be any that keep to these rules, and one draw needn't show every extreme that they name: Each device's 2 lengths sum to at most 128; its tokens are its sequences in slot order, then padding. In every draw some device holds one sequence of 128 tokens and a second slot of 0.
All inputs are finite; a program needn't handle non-finite values.
Results may differ from the reference program's by a relative error of at most 0.015.
Values may be sent and summed in bfloat16 or wider, within the bound.
A program may use at most 192 MiB of HBM per device.

```python
import math
import jax
import jax.numpy as jnp
from jax import lax

HEADS = 12
HEAD_DIM = 64
FF = 3072
TOK_DEV = 128
SEQ_DEV = 2
D = 768
TOKENS = 4096
SLOTS = 64


def draw_lengths(key, part):
    key = jax.random.fold_in(key, 11)
    groups = SLOTS // SEQ_DEV
    key_lead, key_trail, key_full = jax.random.split(key, 3)
    leading = jax.random.randint(key_lead, (groups,), TOK_DEV // 8, TOK_DEV - TOK_DEV // 8 + 1)
    trailing = jax.random.randint(key_trail, (groups,), TOK_DEV // 16, TOK_DEV - leading + 1)
    chosen = jax.random.randint(key_full, (), 0, groups)
    position = jnp.arange(groups)
    leading = jnp.where(position == chosen, TOK_DEV, leading)
    trailing = jnp.where(position == chosen, 0, trailing)
    return jnp.stack([leading, trailing], axis=1).reshape(SLOTS).astype(jnp.int32)


def strengthened(drawn, own_key, source, target, shards_of, factor):
    owner, partner = [(jnp.arange(drawn.shape[dim]) // (drawn.shape[dim] // shards_of)).reshape([-1 if axis == dim else 1 for axis in range(drawn.ndim)]) for dim in (source, target)]
    chosen = jax.random.permutation(own_key, shards_of)[partner]
    strong = (owner == chosen) | (owner == (partner + shards_of // 2) % shards_of)
    return jnp.where(strong, factor * drawn, drawn)


def steps_of(key, extent, cuts, low, high):
    def one(dim, blocks):
        steps = jax.random.uniform(jax.random.fold_in(jax.random.fold_in(key, 6), dim), (blocks,), jnp.float32, low / len(cuts), high / len(cuts))
        return jnp.repeat(jnp.exp(steps), extent[dim] // blocks).reshape((-1,) + (1,) * (len(extent) - dim - 1))

    loudness = one(*cuts[0])
    for cut in cuts[1:]:
        loudness = loudness * one(*cut)
    return loudness


def normal_values(own_key, shape, scale, bound, cuts=(), kind=jnp.bfloat16):
    array = scale * jax.random.normal(own_key, shape, jnp.float32)
    if cuts:
        array = array * steps_of(own_key, shape, cuts, -0.22, 0.18)
    return jnp.clip(array, -bound, bound).astype(kind)


def noise_with(rng, shape, scale, limit, cuts, heavy, kind=jnp.bfloat16):
    values = scale * jax.random.normal(rng, shape, jnp.float32)
    if cuts:
        values = values * steps_of(rng, shape, cuts, -0.22, 0.18)
    return jnp.clip(strengthened(values, jax.random.fold_in(rng, 3), *heavy), -limit, limit).astype(kind)


def setup_inputs(seed: int = 0) -> dict:
    streams_of = jax.random.split(jax.random.key(seed), 17)
    return {
        "tokens": noise_with(streams_of[0], (TOKENS, D), 1.0, 6.0, ((0, 32),), (0, 1, 32, 2.75)),
        "lengths": draw_lengths(jax.random.fold_in(streams_of[16], 71), 0),
        "qkv_weight": normal_values(streams_of[2], (D, 3 * D), D ** -0.5, 0.21875, ((0, 32),)),
        "query_bias": normal_values(streams_of[3], (D,), 0.5, 3.0, ((0, 32),)),
        "value_bias": normal_values(streams_of[4], (D,), 0.5, 3.0, ((0, 32),)),
        "out_weight": normal_values(streams_of[5], (D, D), (D // 16) ** -0.5, 0.875, ((0, 32),)),
        "out_bias": normal_values(streams_of[6], (D,), 0.5, 3.0, ((0, 32),)),
        "norm_one_gain": jnp.clip(1.0 + 0.1 * jax.random.normal(streams_of[7], (D,), jnp.float32), 0.5, 1.5).astype(jnp.bfloat16),
        "norm_one_shift": normal_values(streams_of[8], (D,), 0.5, 3.0, ((0, 32),)),
        "ff_in_weight": normal_values(streams_of[9], (D, FF), D ** -0.5, 0.21875, ((0, 32),)),
        "ff_in_bias": normal_values(streams_of[10], (FF,), 0.5, 3.0, ((0, 32),)),
        "ff_out_weight": normal_values(streams_of[11], (FF, D), FF ** -0.5, 0.109375, ((0, 32),)),
        "ff_out_bias": normal_values(streams_of[12], (D,), 0.5, 3.0, ((0, 32),)),
        "norm_two_gain": jnp.clip(1.0 + 0.1 * jax.random.normal(streams_of[13], (D,), jnp.float32), 0.5, 1.5).astype(jnp.bfloat16),
        "norm_two_shift": normal_values(streams_of[14], (D,), 0.5, 3.0, ((0, 32),)),
        "out_grad": noise_with(streams_of[15], (TOKENS, D), 1.0, 6.0, ((0, 32),), (0, 1, 32, 2.75)),
    }


highest = lax.Precision.HIGHEST

@jax.custom_vjp
def low(v):
    return lax.optimization_barrier(v.astype(jnp.bfloat16)).astype(jnp.float32)

@jax.custom_vjp
def low_back(v):
    return v

def low_keep(v):
    return (low(v), None)

def low_pass(kept, grad):
    return (grad,)

def back_keep(v):
    return (v, None)

def back_low(kept, grad):
    return (low(grad),)
low.defvjp(low_keep, low_pass)
low_back.defvjp(back_keep, back_low)

def layer_norm(hidden, gain, shift):
    center = lax.optimization_barrier(jnp.mean(hidden, axis=-1, keepdims=True))
    centered = hidden - center
    spread = lax.optimization_barrier(jnp.mean(centered * centered, axis=-1, keepdims=True))
    return centered * lax.rsqrt(spread + 1e-06) * gain + shift

def encoder_block(block_tokens, block_segments, params):
    weight_qkv, bias_query, bias_value, weight_out, bias_out, gain_first, shift_first, weight_in, bias_in, weight_down, bias_down, gain_second, shift_second = params
    block_count = block_tokens.shape[0]
    flat_rows = block_tokens.reshape(block_count * TOK_DEV, D)
    zero_keys = jnp.zeros((D,), jnp.float32)
    projected = jnp.dot(flat_rows, weight_qkv, precision=highest) + jnp.concatenate([bias_query, zero_keys, bias_value])
    projected = low_back(low(projected))
    split = projected.reshape(block_count, TOK_DEV, 3, HEADS, HEAD_DIM)
    raw = jnp.einsum('gqhd,gkhd->ghqk', split[:, :, 0], split[:, :, 1], precision=highest) * HEAD_DIM ** (-0.5)
    allowed = block_segments[:, None, :, None] == block_segments[:, None, None, :]
    scores = low_back(jnp.where(allowed, raw, -1e+30))
    attend = low(jax.nn.softmax(scores, axis=-1))
    context = jnp.einsum('ghqk,gkhd->gqhd', attend, split[:, :, 2], precision=highest)
    context = low_back(low(context.reshape(block_count * TOK_DEV, D)))
    attn_out = low_back(jnp.dot(context, weight_out, precision=highest) + bias_out)
    first_norm = layer_norm(flat_rows + attn_out, gain_first, shift_first)
    pre_act = low_back(jnp.dot(low(first_norm), weight_in, precision=highest) + bias_in)
    activated = low(jax.nn.gelu(pre_act, approximate=False))
    ff_result = low_back(jnp.dot(activated, weight_down, precision=highest) + bias_down)
    encoded = layer_norm(first_norm + ff_result, gain_second, shift_second)
    return encoded.reshape(block_tokens.shape)

def reference(tokens, lengths, qkv_weight, query_bias, value_bias, out_weight, out_bias, norm_one_gain, norm_one_shift, ff_in_weight, ff_in_bias, ff_out_weight, ff_out_bias, norm_two_gain, norm_two_shift, out_grad):
    groups = lengths.shape[0] // SEQ_DEV
    per_block = math.gcd(groups, max(1, 4096 // TOK_DEV))
    bounds = jnp.cumsum(lengths.reshape(groups, SEQ_DEV), axis=1).astype(jnp.int32)
    position = jnp.arange(TOK_DEV, dtype=jnp.int32)
    segments = lax.optimization_barrier(jnp.sum((position[None, :, None] >= bounds[:, None, :]).astype(jnp.int32), axis=2))
    segments = segments.reshape(groups // per_block, per_block, TOK_DEV)
    params = tuple((w.astype(jnp.float32) for w in (qkv_weight, query_bias, value_bias, out_weight, out_bias, norm_one_gain, norm_one_shift, ff_in_weight, ff_in_bias, ff_out_weight, ff_out_bias, norm_two_gain, norm_two_shift)))
    blocks_in = tokens.astype(jnp.float32).reshape(groups // per_block, per_block, TOK_DEV, D)

    def forward(block_inputs, weights):

        def one_block(pair):
            return encoder_block(pair[0], pair[1], weights)
        return lax.map(jax.checkpoint(one_block), (block_inputs, segments))
    result, pullback = jax.vjp(forward, blocks_in, params)
    grad_blocks, grad_params = pullback(out_grad.astype(jnp.float32).reshape(result.shape))
    encoded = result.reshape(TOKENS, D).astype(jnp.bfloat16)
    return (encoded, grad_blocks.reshape(TOKENS, D), grad_params[0], grad_params[1], grad_params[2], grad_params[3], grad_params[4], grad_params[5], grad_params[6], grad_params[7], grad_params[8], grad_params[9], grad_params[10], grad_params[11], grad_params[12])
```

```python
import functools

import jax
import jax.numpy as jnp
from jax import lax
from jax.experimental import pallas as pl
from jax.experimental.pallas import tpu as pltpu
from jax.sharding import PartitionSpec as P

HEAD_DIM = 64
SMALL_ROWS = 16
LANES = 128
VMEM_BYTES = 56 * 1024 * 1024
MESH = pl.DeviceIdType.MESH


class Place:
    def __init__(self, devices, core=None):
        self.chips = devices // 2
        side = max(s for s in range(1, self.chips + 1) if s**3 <= self.chips and self.chips % (s * s) == 0)
        self.side = side
        self.depth = self.chips // (side * side)
        me = lax.axis_index("dp")
        self.chip = me // 2
        self.own_core = lax.rem(me, 2)
        self.core = self.own_core if core is None else core(self.own_core)
        first = self.core == 0
        self.step_a = side * side
        self.step_s = jnp.where(first, side, 1)
        self.step_t = jnp.where(first, 1, side)
        self.pos_a = self.chip // self.step_a
        mid = lax.rem(self.chip // side, side)
        low = lax.rem(self.chip, side)
        self.pos_s = jnp.where(first, mid, low)
        self.pos_t = jnp.where(first, low, mid)

    def at(self, da, ds, dt):
        a = lax.rem(self.pos_a + da, self.depth)
        s = lax.rem(self.pos_s + ds, self.side)
        t = lax.rem(self.pos_t + dt, self.side)
        return a * self.step_a + s * self.step_s + t * self.step_t

    def device(self, da, ds, dt):
        return self.at(da, ds, dt) * 2 + self.own_core

    def sibling(self):
        return self.chip * 2 + 1 - self.own_core

    def peers(self):
        found = [self.sibling()]
        found += [self.device(d, 0, 0) for d in range(1, self.depth)]
        found += [self.device(0, d, 0) for d in range(1, self.side)]
        found += [self.device(0, 0, d) for d in range(1, self.side)]
        return found


def greet(place):
    barrier = pltpu.get_barrier_semaphore()
    peers = place.peers()
    for peer in peers:
        pl.semaphore_signal(barrier, inc=1, device_id=(peer,), device_id_type=MESH)
    pl.semaphore_wait(barrier, len(peers))


def gather_kernel(devices, count, *refs):
    shards, fulls = refs[:count], refs[count : 2 * count]
    (send_a, recv_a, send_s, recv_s, send_t, recv_t, send_c, recv_c, own_sem) = refs[2 * count :]
    place = Place(devices)
    depth, side = place.depth, place.side
    core = place.core
    greet(place)
    started = []

    def send(source, full, chip, ssem, rsem, device):
        copy = pltpu.make_async_remote_copy(
            src_ref=source, dst_ref=full.at[chip, core], send_sem=ssem, recv_sem=rsem,
            device_id=(device,), device_id_type=MESH)
        copy.start()
        started.append(copy)

    def arrived(w, chip, rsem, from_core):
        full = fulls[w]
        pltpu.make_async_remote_copy(
            src_ref=full.at[chip, from_core], dst_ref=full.at[chip, from_core], send_sem=rsem, recv_sem=rsem,
            device_id=(place.sibling(),), device_id_type=MESH).wait_recv()

    def pass_on(w, source, chip, da, ds, dt, to_s, to_t):
        full = fulls[w]
        if to_t:
            for d in range(1, side):
                at = da * side + ds
                send(source, full, chip, send_t.at[w, d - 1, at], recv_t.at[w, d - 1, at], place.device(0, 0, d))
        if to_s:
            for d in range(1, side):
                send(source, full, chip, send_s.at[w, d - 1, da], recv_s.at[w, d - 1, da], place.device(0, d, 0))
        at = (da * side + ds) * side + dt
        send(source, full, chip, send_c.at[w, at], recv_c.at[w, at], place.sibling())

    own = place.at(0, 0, 0)
    own_copies = []
    for w in range(count):
        for d in range(1, depth):
            send(shards[w], fulls[w], own, send_a.at[w, d - 1], recv_a.at[w, d - 1], place.device(d, 0, 0))
        pass_on(w, shards[w], own, 0, 0, 0, True, True)
        local = pltpu.make_async_copy(shards[w], fulls[w].at[own, core], own_sem.at[w])
        local.start()
        own_copies.append(local)
    for da in range(1, depth):
        for w in range(count):
            chip = place.at(depth - da, 0, 0)
            arrived(w, chip, recv_a.at[w, da - 1], core)
            pass_on(w, fulls[w].at[chip, core], chip, da, 0, 0, True, True)
    for da in range(depth):
        for ds in range(1, side):
            for w in range(count):
                chip = place.at((depth - da) % depth, side - ds, 0)
                arrived(w, chip, recv_s.at[w, ds - 1, da], core)
                pass_on(w, fulls[w].at[chip, core], chip, da, ds, 0, False, True)
    for da in range(depth):
        for ds in range(side):
            for dt in range(1, side):
                for w in range(count):
                    chip = place.at((depth - da) % depth, (side - ds) % side, side - dt)
                    arrived(w, chip, recv_t.at[w, dt - 1, da * side + ds], core)
                    pass_on(w, fulls[w].at[chip, core], chip, da, ds, dt, False, False)
    other = Place(devices, lambda own_core: 1 - own_core)
    for da in range(depth):
        for ds in range(side):
            for dt in range(side):
                for w in range(count):
                    chip = other.at((depth - da) % depth, (side - ds) % side, (side - dt) % side)
                    arrived(w, chip, recv_c.at[w, (da * side + ds) * side + dt], 1 - core)
    for copy in started:
        copy.wait_send()
    for local in own_copies:
        local.wait()


def gather_all(shards, devices):
    chips = devices // 2
    side = max(s for s in range(1, chips + 1) if s**3 <= chips and chips % (s * s) == 0)
    depth = chips // (side * side)
    count = len(shards)
    dma = pltpu.SemaphoreType.DMA
    vmem = pl.BlockSpec(memory_space=pltpu.VMEM)
    pairs = [(count, depth - 1), (count, side - 1, depth), (count, side - 1, depth * side), (count, chips)]
    scratch = []
    for shape in pairs:
        scratch += [dma(shape), dma(shape)]
    return pl.pallas_call(
        functools.partial(gather_kernel, devices, count),
        out_shape=[jax.ShapeDtypeStruct((chips, 2) + s.shape, s.dtype) for s in shards],
        in_specs=[vmem] * count,
        out_specs=[vmem] * count,
        scratch_shapes=scratch + [dma((count,))],
        compiler_params=pltpu.CompilerParams(
            collective_id=0, has_side_effects=True, vmem_limit_bytes=VMEM_BYTES),
        cost_estimate=pl.CostEstimate(flops=0, bytes_accessed=16_000_000, transcendentals=0),
        name="gather_parameters",
    )(*shards)


def scatter_kernel(devices, count, *refs):
    parts, outs = refs[:count], refs[count : 2 * count]
    held = refs[2 * count : 3 * count]
    from_t = refs[3 * count : 4 * count]
    from_s = refs[4 * count : 5 * count]
    from_a = refs[5 * count : 6 * count]
    (send_a, recv_a, send_s, recv_s, send_t, recv_t, send_c, recv_c) = refs[6 * count :]
    place = Place(devices)
    other = Place(devices, lambda own_core: 1 - own_core)
    depth, side = place.depth, place.side
    core = place.core
    greet(place)
    started = []

    def send(source, target, ssem, rsem, device):
        copy = pltpu.make_async_remote_copy(
            src_ref=source, dst_ref=target, send_sem=ssem, recv_sem=rsem,
            device_id=(device,), device_id_type=MESH)
        copy.start()
        started.append(copy)

    def arrived(target, rsem):
        pltpu.make_async_remote_copy(
            src_ref=target, dst_ref=target, send_sem=rsem, recv_sem=rsem,
            device_id=(place.sibling(),), device_id_type=MESH).wait_recv()

    order = [(da, ds, dt) for dt in range(1, side) for ds in list(range(1, side)) + [0] for da in list(range(1, depth)) + [0]]
    order += [(da, ds, 0) for ds in range(1, side) for da in list(range(1, depth)) + [0]]
    order += [(da, 0, 0) for da in list(range(1, depth)) + [0]]

    def number(da, ds, dt):
        return (da * side + ds) * side + dt

    for w in range(count):
        for da, ds, dt in order:
            chip = other.at(da, ds, dt)
            at = number(da, ds, dt)
            send(parts[w].at[chip, 1 - core], held[w].at[chip], send_c.at[w, at], recv_c.at[w, at], place.sibling())

    def collect(w, da, ds, dt):
        chip = place.at(da, ds, dt)
        arrived(held[w].at[chip], recv_c.at[w, number(da, ds, dt)])
        total = parts[w][chip, core].astype(jnp.float32) + held[w][chip].astype(jnp.float32)
        if dt == 0:
            for d in range(1, side):
                at = da * side + ds
                arrived(from_t[w].at[d - 1, at], recv_t.at[w, d - 1, at])
                total = total + from_t[w][d - 1, at].astype(jnp.float32)
            if ds == 0:
                for d in range(1, side):
                    arrived(from_s[w].at[d - 1, da], recv_s.at[w, d - 1, da])
                    total = total + from_s[w][d - 1, da].astype(jnp.float32)
                if da == 0:
                    for d in range(1, depth):
                        arrived(from_a[w].at[d - 1], recv_a.at[w, d - 1])
                        total = total + from_a[w][d - 1].astype(jnp.float32)
        return chip, total

    for dt in range(1, side):
        for w in range(count):
            for ds in list(range(1, side)) + [0]:
                for da in list(range(1, depth)) + [0]:
                    chip, total = collect(w, da, ds, dt)
                    held[w][chip] = total.astype(held[w].dtype)
                    at = da * side + ds
                    send(held[w].at[chip], from_t[w].at[dt - 1, at], send_t.at[w, dt - 1, at],
                         recv_t.at[w, dt - 1, at], place.device(0, 0, dt))
    for ds in range(1, side):
        for w in range(count):
            for da in list(range(1, depth)) + [0]:
                chip, total = collect(w, da, ds, 0)
                held[w][chip] = total.astype(held[w].dtype)
                send(held[w].at[chip], from_s[w].at[ds - 1, da], send_s.at[w, ds - 1, da],
                     recv_s.at[w, ds - 1, da], place.device(0, ds, 0))
    for w in range(count):
        for da in range(1, depth):
            chip, total = collect(w, da, 0, 0)
            held[w][chip] = total.astype(held[w].dtype)
            send(held[w].at[chip], from_a[w].at[da - 1], send_a.at[w, da - 1],
                 recv_a.at[w, da - 1], place.device(da, 0, 0))
    for w in range(count):
        outs[w][...] = collect(w, 0, 0, 0)[1]
    for copy in started:
        copy.wait_send()


def scatter_all(parts, devices):
    chips = devices // 2
    side = max(s for s in range(1, chips + 1) if s**3 <= chips and chips % (s * s) == 0)
    depth = chips // (side * side)
    count = len(parts)
    dma = pltpu.SemaphoreType.DMA
    vmem = pl.BlockSpec(memory_space=pltpu.VMEM)
    pairs = [(count, depth - 1), (count, side - 1, depth), (count, side - 1, depth * side), (count, chips)]
    scratch = []
    for lead in ((chips,), (side - 1, depth * side), (side - 1, depth), (depth - 1,)):
        scratch += [pltpu.VMEM(lead + p.shape[2:], p.dtype) for p in parts]
    for shape in pairs:
        scratch += [dma(shape), dma(shape)]
    return pl.pallas_call(
        functools.partial(scatter_kernel, devices, count),
        out_shape=[jax.ShapeDtypeStruct(p.shape[2:], jnp.float32) for p in parts],
        in_specs=[vmem] * count,
        out_specs=[vmem] * count,
        scratch_shapes=scratch,
        compiler_params=pltpu.CompilerParams(
            collective_id=1, has_side_effects=True, vmem_limit_bytes=VMEM_BYTES),
        cost_estimate=pl.CostEstimate(flops=0, bytes_accessed=16_000_000, transcendentals=0),
        name="scatter_gradients",
    )(*parts)


def pack_rows(vectors, blocks, dtype):
    rows = []
    for v in vectors:
        piece = v.astype(dtype).reshape(blocks, 1, -1)
        rows.append(jnp.pad(piece, ((0, 0), (0, 0), (0, LANES - piece.shape[2]))))
    rows.append(jnp.zeros((blocks, SMALL_ROWS - len(vectors), LANES), dtype))
    return jnp.concatenate(rows, axis=1)


def unpack_rows(packed, lengths):
    return [packed[:, j, :n].reshape(-1) for j, n in enumerate(lengths)]


def gather_params(matrices, vectors, devices):
    lengths = [v.shape[0] for v in vectors]
    small = pack_rows(vectors, 1, jnp.bfloat16)[0]
    if devices > 32:
        full = [lax.all_gather(m, "dp", axis=0, tiled=True) for m in matrices]
        small_full = lax.all_gather(small, "dp", axis=0)
        return full, unpack_rows(small_full, lengths)
    *gathered, small_full = gather_all([*matrices, small], devices)
    full = [g.reshape(devices * m.shape[0], m.shape[1]) for g, m in zip(gathered, matrices)]
    return full, unpack_rows(small_full.reshape(devices, SMALL_ROWS, LANES), lengths)


def scatter_grads(matrices, vectors, devices):
    lengths = [v.shape[0] // devices for v in vectors]
    small = pack_rows(vectors, devices, jnp.float32)
    if devices > 32:
        owned = [lax.psum_scatter(m, "dp", scatter_dimension=0, tiled=True) for m in matrices]
        small_owned = lax.psum_scatter(small, "dp", scatter_dimension=0, tiled=True)[0]
    else:
        chips = devices // 2
        low = [to_low(m).reshape(chips, 2, m.shape[0] // devices, m.shape[1]) for m in matrices]
        small = small.reshape(chips, 2, SMALL_ROWS, LANES)
        *owned, small_owned = scatter_all([*low, small], devices)
    return owned, [small_owned[j, :n] for j, n in enumerate(lengths)]


def layer_norm(hidden, gain, shift):
    center = jnp.mean(hidden, axis=-1, keepdims=True)
    centered = hidden - center
    spread = jnp.mean(centered * centered, axis=-1, keepdims=True)
    return centered * lax.rsqrt(spread + 1e-06) * gain + shift


def gelu_exact(values):
    return jax.nn.gelu(values, approximate=False)


def to_low(values):
    return values.astype(jnp.bfloat16)


def as_float(values):
    return values.astype(jnp.float32)


def matmul(left, right):
    return jnp.dot(left, right, preferred_element_type=jnp.float32)


def matmul_left_t(left, right):
    return lax.dot_general(
        left, right, (((0,), (0,)), ((), ())), preferred_element_type=jnp.float32
    )


def matmul_right_t(left, right):
    return lax.dot_general(
        left, right, (((1,), (1,)), ((), ())), preferred_element_type=jnp.float32
    )


def masked_scores(queries, keys, allowed):
    raw = jnp.einsum(
        "hqd,hkd->hqk", queries, keys, preferred_element_type=jnp.float32
    ) * HEAD_DIM ** (-0.5)
    return jnp.where(allowed[None], raw, -1e30)


def body(
    tokens,
    lengths,
    qkv_weight,
    query_bias,
    value_bias,
    out_weight,
    out_bias,
    norm_one_gain,
    norm_one_shift,
    ff_in_weight,
    ff_in_bias,
    ff_out_weight,
    ff_out_bias,
    norm_two_gain,
    norm_two_shift,
    out_grad,
):
    rows, width = tokens.shape
    heads = width // HEAD_DIM
    scale = HEAD_DIM ** (-0.5)
    devices = lax.axis_size("dp")
    (weight_qkv, weight_out, weight_in, weight_down), vectors = gather_params(
        (qkv_weight, out_weight, ff_in_weight, ff_out_weight),
        (
            query_bias,
            value_bias,
            out_bias,
            norm_one_gain,
            norm_one_shift,
            ff_out_bias,
            norm_two_gain,
            norm_two_shift,
            ff_in_bias,
        ),
        devices,
    )
    (bias_query, bias_value, bias_out, gain_first, shift_first, bias_down, gain_second,
     shift_second, bias_in) = vectors
    bounds = jnp.cumsum(lengths)
    position = jnp.arange(rows, dtype=jnp.int32)
    segments = jnp.sum((position[:, None] >= bounds[None, :]).astype(jnp.int32), axis=1)
    allowed = segments[:, None] == segments[None, :]
    zero_keys = jnp.zeros((width,), jnp.float32)
    qkv_bias = jnp.concatenate([as_float(bias_query), zero_keys, as_float(bias_value)])
    projected = to_low(matmul(tokens, weight_qkv) + qkv_bias)
    split = projected.reshape(rows, 3, heads, HEAD_DIM).transpose(1, 2, 0, 3)
    queries, keys, values = (split[0], split[1], split[2])
    scores = masked_scores(queries, keys, allowed)
    peak = jnp.max(scores, axis=-1, keepdims=True)
    log_total = peak + jnp.log(jnp.sum(jnp.exp(scores - peak), axis=-1, keepdims=True))
    attend = jnp.exp(scores - log_total)
    context = jnp.einsum("hqk,hkd->qhd", to_low(attend), values, preferred_element_type=jnp.float32)
    context = to_low(context.reshape(rows, width))
    first_sum = as_float(tokens) + matmul(context, weight_out) + as_float(bias_out)
    first_norm, norm_one_pull = jax.vjp(
        layer_norm, first_sum, as_float(gain_first), as_float(shift_first)
    )
    first_low = to_low(first_norm)
    pre_act = matmul(first_low, weight_in) + as_float(bias_in)
    activated = to_low(gelu_exact(pre_act))
    second_sum = first_norm + matmul(activated, weight_down) + as_float(bias_down)
    encoded, norm_two_pull = jax.vjp(
        layer_norm, second_sum, as_float(gain_second), as_float(shift_second)
    )
    grad_second, grad_gain_second, grad_shift_second = norm_two_pull(as_float(out_grad))
    grad_ff = to_low(grad_second)
    grad_weight_down = matmul_left_t(activated, grad_ff)
    grad_bias_down = jnp.sum(as_float(grad_ff), axis=0)
    grad_act = matmul_right_t(grad_ff, weight_down)
    gelu_pull = jax.vjp(gelu_exact, pre_act)[1]
    grad_pre = to_low(gelu_pull(grad_act)[0])
    grad_weight_in = matmul_left_t(first_low, grad_pre)
    grad_bias_in = jnp.sum(as_float(grad_pre), axis=0)
    grad_first = grad_second + matmul_right_t(grad_pre, weight_in)
    grad_first_sum, grad_gain_first, grad_shift_first = norm_one_pull(grad_first)
    grad_attn = to_low(grad_first_sum)
    grad_weight_out = matmul_left_t(context, grad_attn)
    grad_bias_out = jnp.sum(as_float(grad_attn), axis=0)
    grad_context = to_low(matmul_right_t(grad_attn, weight_out))
    grad_heads = grad_context.reshape(rows, heads, HEAD_DIM).transpose(1, 0, 2)
    again_scores = masked_scores(queries, keys, allowed)
    again_attend = jnp.exp(again_scores - log_total)
    grad_values = jnp.einsum(
        "hqk,hqd->hkd", to_low(again_attend), grad_heads, preferred_element_type=jnp.float32
    )
    grad_attend = jnp.einsum("hqd,hkd->hqk", grad_heads, values, preferred_element_type=jnp.float32)
    row_total = jnp.sum(grad_attend * again_attend, axis=-1, keepdims=True)
    grad_scores = to_low(again_attend * (grad_attend - row_total))
    grad_queries = (
        jnp.einsum("hqk,hkd->hqd", grad_scores, keys, preferred_element_type=jnp.float32) * scale
    )
    grad_keys = (
        jnp.einsum("hqk,hqd->hkd", grad_scores, queries, preferred_element_type=jnp.float32) * scale
    )
    grad_qkv = to_low(
        jnp.stack([grad_queries, grad_keys, grad_values])
        .transpose(2, 0, 1, 3)
        .reshape(rows, 3 * width)
    )
    grad_weight_qkv = matmul_left_t(tokens, grad_qkv)
    grad_columns = jnp.sum(as_float(grad_qkv), axis=0)
    grad_bias_query = grad_columns[:width]
    grad_bias_value = grad_columns[2 * width :]
    grad_tokens = grad_first_sum + matmul_right_t(grad_qkv, weight_qkv)
    (own_down, own_in, own_out, own_qkv), own = scatter_grads(
        (grad_weight_down, grad_weight_in, grad_weight_out, grad_weight_qkv),
        (
            grad_bias_query,
            grad_bias_value,
            grad_bias_out,
            grad_gain_first,
            grad_shift_first,
            grad_bias_down,
            grad_gain_second,
            grad_shift_second,
            grad_bias_in,
        ),
        devices,
    )
    return (
        to_low(encoded),
        grad_tokens,
        own_qkv,
        own[0],
        own[1],
        own_out,
        own[2],
        own[3],
        own[4],
        own_in,
        own[8],
        own_down,
        own[5],
        own[6],
        own[7],
    )


def solution(mesh):
    in_specs = (
        P("dp", None),
        P("dp"),
        P("dp", None),
        P("dp"),
        P("dp"),
        P("dp", None),
        P("dp"),
        P("dp"),
        P("dp"),
        P("dp", None),
        P("dp"),
        P("dp", None),
        P("dp"),
        P("dp"),
        P("dp"),
        P("dp", None),
    )
    out_specs = (
        P("dp", None),
        P("dp", None),
        P("dp", None),
        P("dp"),
        P("dp"),
        P("dp", None),
        P("dp"),
        P("dp"),
        P("dp"),
        P("dp", None),
        P("dp"),
        P("dp", None),
        P("dp"),
        P("dp"),
        P("dp"),
    )
    return jax.shard_map(body, mesh=mesh, in_specs=in_specs, out_specs=out_specs, check_vma=False)
```

```python
from types import SimpleNamespace

import jax
import jax.numpy as jnp
from jax import lax
from jax.experimental import pallas as pl
from jax.experimental.pallas import tpu as pltpu
from jax.sharding import PartitionSpec as P

HEAD_DIM = 64
SMALL_ROWS = 16
LANES = 128
VMEM_BYTES = 60 * 1024 * 1024
MESH = pl.DeviceIdType.MESH


class Place:
    def __init__(self, devices, core=None):
        self.chips = devices // 2
        side = max(s for s in range(1, self.chips + 1) if s**3 <= self.chips and self.chips % (s * s) == 0)
        self.side = side
        self.depth = self.chips // (side * side)
        me = lax.axis_index("dp")
        self.chip = me // 2
        self.own_core = lax.rem(me, 2)
        self.core = self.own_core if core is None else core(self.own_core)
        first = self.core == 0
        self.step_a = side * side
        self.step_s = jnp.where(first, side, 1)
        self.step_t = jnp.where(first, 1, side)
        self.pos_a = self.chip // self.step_a
        mid = lax.rem(self.chip // side, side)
        low = lax.rem(self.chip, side)
        self.pos_s = jnp.where(first, mid, low)
        self.pos_t = jnp.where(first, low, mid)

    def at(self, da, ds, dt):
        a = lax.rem(self.pos_a + da, self.depth)
        s = lax.rem(self.pos_s + ds, self.side)
        t = lax.rem(self.pos_t + dt, self.side)
        return a * self.step_a + s * self.step_s + t * self.step_t

    def device(self, da, ds, dt):
        return self.at(da, ds, dt) * 2 + self.own_core

    def sibling(self):
        return self.chip * 2 + 1 - self.own_core

    def peers(self):
        found = [self.sibling()]
        found += [self.device(d, 0, 0) for d in range(1, self.depth)]
        found += [self.device(0, d, 0) for d in range(1, self.side)]
        found += [self.device(0, 0, d) for d in range(1, self.side)]
        return found


def greet(place):
    barrier = pltpu.get_barrier_semaphore()
    peers = place.peers()
    for peer in peers:
        pl.semaphore_signal(barrier, inc=1, device_id=(peer,), device_id_type=MESH)
    pl.semaphore_wait(barrier, len(peers))


WEIGHTS = 4
VECTORS = 9
CHUNK = 384


def dot(left, right):
    return jnp.dot(left, right, preferred_element_type=jnp.float32)


def dot_nt(left, right):
    return lax.dot_general(left, right, (((1,), (1,)), ((), ())), preferred_element_type=jnp.float32)


def dot_tn(left, right):
    return lax.dot_general(left, right, (((0,), (0,)), ((), ())), preferred_element_type=jnp.float32)


def erf_rational(x):
    x = jnp.clip(x, -3.832506856900711, 3.832506856900711)
    y = x * x
    top = jnp.full_like(y, 0.00022905065861350646)
    for c in (0.0034082910107109506, 0.050955695062380861, 0.18520832239976145, 1.128379143519084):
        top = top * y + c
    low = jnp.full_like(y, -1.1791602954361697e-7)
    for c in (0.000023547966471313185, 0.0010179625278914885, 0.014070470171167667,
              0.11098505178285362, 0.49746925110067538, 1.0):
        low = low * y + c
    return x * top / low


def norm_parts(hidden):
    center = jnp.mean(hidden, axis=-1, keepdims=True)
    centered = hidden - center
    inverse = lax.rsqrt(jnp.mean(centered * centered, axis=-1, keepdims=True) + 1e-06)
    return centered * inverse, inverse


def norm_back(grad, gain, unit, inverse):
    scaled = grad * gain
    mean_one = jnp.mean(scaled, axis=-1, keepdims=True)
    mean_two = jnp.mean(scaled * unit, axis=-1, keepdims=True)
    return inverse * (scaled - mean_one - unit * mean_two)


def column_sum(values):
    return jnp.sum(values, axis=0, keepdims=True)


def lane_owner(rows, columns, piece):
    row = lax.broadcasted_iota(jnp.int32, (rows, columns), 0)
    column = lax.broadcasted_iota(jnp.int32, (rows, columns), 1)
    return (lax.rem(column, piece) == row).astype(jnp.bfloat16)


def owner_mask(devices, repeat, columns, piece):
    row = lax.broadcasted_iota(jnp.int32, (devices * repeat, columns), 0)
    column = lax.broadcasted_iota(jnp.int32, (devices * repeat, columns), 1)
    start = (row // repeat) * piece
    return jnp.logical_and(column >= start, column < start + piece)


def layer_kernel(devices, ref):
    place = Place(devices)
    other = Place(devices, lambda own_core: 1 - own_core)
    depth, side, core = place.depth, place.side, place.core
    chips = devices // 2
    sibling = place.sibling()
    count = WEIGHTS + 1
    weights = ref.weight
    grads = ref.grad
    held = ref.held
    from_t = ref.from_t
    from_s = ref.from_s
    from_a = ref.from_a
    shards = ref.shard
    raws = ref.raw
    started = []

    def send(source, target, ssem, rsem, device):
        copy = pltpu.make_async_remote_copy(
            src_ref=source, dst_ref=target, send_sem=ssem, recv_sem=rsem,
            device_id=(device,), device_id_type=MESH)
        copy.start()
        started.append(copy)

    def arrived(target, rsem):
        pltpu.make_async_remote_copy(
            src_ref=target, dst_ref=target, send_sem=rsem, recv_sem=rsem,
            device_id=(sibling,), device_id_type=MESH).wait_recv()

    def rows_of(w, chip):
        rows = 2 * shards[w].shape[0]
        return pl.ds(pl.multiple_of(chip * rows, rows), rows)

    def block(array, w, chip, of_core):
        if w == WEIGHTS:
            return array.at[chip, of_core]
        return array.at[of_core, rows_of(w, chip)]

    own = place.at(0, 0, 0)
    piece = ref.vector[0].shape[1]
    wide = ref.vector[8].shape[1]
    pack = ref.pack
    pack[...] = jnp.zeros_like(pack)
    for j in range(VECTORS):
        v = ref.vector[j]
        pack[j : j + 1, 0 : v.shape[1]] = v[...].astype(jnp.float32)
    weights[WEIGHTS][own, core] = pack[...]
    greet(place)
    for w in range(WEIGHTS):
        send(shards[w], raws[w], ref.raw_send.at[w], ref.raw_recv.at[w], sibling)

    def pass_on(w, chip, da, ds, dt, to_s, to_t):
        part = block(weights[w], w, chip, core)
        if to_t:
            for d in range(1, side):
                at = da * side + ds
                send(part, part, ref.g_send_t.at[w, d - 1, at], ref.g_recv_t.at[w, d - 1, at], place.device(0, 0, d))
        if to_s:
            for d in range(1, side):
                send(part, part, ref.g_send_s.at[w, d - 1, da], ref.g_recv_s.at[w, d - 1, da], place.device(0, d, 0))
        if (da, ds, dt) != (0, 0, 0) or w == WEIGHTS:
            at = (da * side + ds) * side + dt
            send(part, part, ref.g_send_c.at[w, at], ref.g_recv_c.at[w, at], sibling)

    def gather_own(w):
        if w < WEIGHTS:
            arrived(raws[w], ref.raw_recv.at[w])
            mine = shards[w][...].astype(jnp.float32)
            theirs = raws[w][...].astype(jnp.float32)
            both = jnp.concatenate(
                [jnp.where(core == 0, mine, theirs), jnp.where(core == 0, theirs, mine)], axis=0).astype(jnp.bfloat16)
            half = both.shape[1] // 2
            weights[w][0, rows_of(w, own)] = both[:, :half]
            weights[w][1, rows_of(w, own)] = both[:, half:]
        part = block(weights[w], w, own, core)
        for d in range(1, depth):
            send(part, part, ref.g_send_a.at[w, d - 1], ref.g_recv_a.at[w, d - 1], place.device(d, 0, 0))
        pass_on(w, own, 0, 0, 0, True, True)

    def gather_a(w):
        for da in range(1, depth):
            chip = place.at(depth - da, 0, 0)
            arrived(block(weights[w], w, chip, core), ref.g_recv_a.at[w, da - 1])
            pass_on(w, chip, da, 0, 0, True, True)

    def gather_s(w):
        for da in range(depth):
            for ds in range(1, side):
                chip = place.at((depth - da) % depth, side - ds, 0)
                arrived(block(weights[w], w, chip, core), ref.g_recv_s.at[w, ds - 1, da])
                pass_on(w, chip, da, ds, 0, False, True)

    def gather_t(w):
        for da in range(depth):
            for ds in range(side):
                for dt in range(1, side):
                    chip = place.at((depth - da) % depth, (side - ds) % side, side - dt)
                    arrived(block(weights[w], w, chip, core), ref.g_recv_t.at[w, dt - 1, da * side + ds])
                    pass_on(w, chip, da, ds, dt, False, False)

    def gather_c(w):
        for da in range(depth):
            for ds in range(side):
                for dt in range(side):
                    if (da, ds, dt) == (0, 0, 0) and w < WEIGHTS:
                        continue
                    chip = other.at((depth - da) % depth, (side - ds) % side, (side - dt) % side)
                    arrived(block(weights[w], w, chip, 1 - core),
                            ref.g_recv_c.at[w, (da * side + ds) * side + dt])

    arrivals = (WEIGHTS, 0, 1, 2, 3)
    for w in arrivals:
        gather_own(w)
    for w in arrivals:
        gather_a(w)
    for w in arrivals:
        gather_s(w)

    tokens = ref.tokens
    rows, width = tokens.shape
    hidden = weights[2].shape[2] * 2
    heads = width // HEAD_DIM
    scale = HEAD_DIM ** (-0.5)
    qkv, context = ref.qkv, ref.context
    ref.tokens_t[...] = tokens[...].T
    position_r = lax.broadcasted_iota(jnp.int32, (rows, rows), 0)
    position_c = lax.broadcasted_iota(jnp.int32, (rows, rows), 1)
    segment_r = jnp.zeros((rows, rows), jnp.int32)
    segment_c = jnp.zeros((rows, rows), jnp.int32)
    bound = jnp.int32(0)
    for slot in range(ref.lengths.shape[0]):
        bound = bound + ref.lengths[slot]
        segment_r = segment_r + (position_r >= bound).astype(jnp.int32)
        segment_c = segment_c + (position_c >= bound).astype(jnp.int32)
    allowed = segment_r == segment_c

    gather_t(WEIGHTS)
    gather_c(WEIGHTS)
    packed = weights[WEIGHTS][...].reshape(devices * SMALL_ROWS, LANES)
    spread = dot(packed.astype(jnp.bfloat16), lane_owner(LANES, width, piece))
    spread = jnp.where(owner_mask(devices, SMALL_ROWS, width, piece), spread, 0.0)
    pick = lane_owner(SMALL_ROWS, devices * SMALL_ROWS, SMALL_ROWS)
    vectors = dot(pick, spread.astype(jnp.bfloat16))
    ninth = dot(weights[WEIGHTS][...].reshape(devices, SMALL_ROWS, LANES)[:, VECTORS - 1, :].astype(jnp.bfloat16),
                lane_owner(LANES, hidden, wide))
    bias_in = column_sum(jnp.where(owner_mask(devices, 1, hidden, wide), ninth, 0.0))
    bias_query, bias_value, bias_out, gain_first, shift_first, bias_down, gain_second, shift_second = [
        vectors[j : j + 1] for j in range(8)]
    qkv_bias = jnp.concatenate([bias_query, jnp.zeros_like(bias_query), bias_value], axis=1)

    gather_t(0)
    gather_c(0)
    half = weights[0].shape[2]
    for h in range(2):
        for c in range(0, half, CHUNK):
            at = h * half + c
            out = dot(tokens[...], weights[0][h, :, c : c + CHUNK]) + qkv_bias[:, at : at + CHUNK]
            qkv[:, at : at + CHUNK] = out.astype(jnp.bfloat16)
    for pair in range(heads // 2):
        found = []
        for h in (2 * pair, 2 * pair + 1):
            q, k, v = [qkv[:, i * width + h * HEAD_DIM : i * width + (h + 1) * HEAD_DIM] for i in range(3)]
            scores = jnp.where(allowed, dot_nt(q, k) * scale, -1e30)
            weight = jnp.exp(scores - jnp.max(scores, axis=-1, keepdims=True))
            weight = weight / jnp.sum(weight, axis=-1, keepdims=True)
            ref.attend[h] = weight
            found.append(dot(weight.astype(jnp.bfloat16), v))
        at = pair * 2 * HEAD_DIM
        context[:, at : at + 2 * HEAD_DIM] = jnp.concatenate(found, axis=1).astype(jnp.bfloat16)
    ref.context_t[...] = context[...].T

    gather_t(1)
    gather_t(2)
    gather_c(1)
    attn = jnp.concatenate([dot(context[...], weights[1][h]) for h in range(2)], axis=1)
    unit_one, inverse_one = norm_parts(tokens[...].astype(jnp.float32) + attn + bias_out)
    ref.unit_one[...] = unit_one
    first_norm = unit_one * gain_first + shift_first
    ref.first_norm[...] = first_norm
    first_low = first_norm.astype(jnp.bfloat16)
    ref.first_low[...] = first_low
    ref.first_t[...] = first_low.T
    gather_t(3)
    gather_c(2)
    half = weights[2].shape[2]
    for h in range(2):
        for c in range(0, half, CHUNK):
            at = h * half + c
            pre = dot(ref.first_low[...], weights[2][h, :, c : c + CHUNK]) + bias_in[:, at : at + CHUNK]
            gate = 0.5 + 0.5 * erf_rational(pre * (0.5**0.5))
            act = (pre * gate).astype(jnp.bfloat16)
            ref.active[:, at : at + CHUNK] = act
            ref.active_t[at : at + CHUNK, :] = act.T
            ref.slope[:, at : at + CHUNK] = gate + pre * (0.3989422804014327 * jnp.exp(-0.5 * pre * pre))
    gather_c(3)
    down = jnp.concatenate([dot(ref.active[...], weights[3][h]) for h in range(2)], axis=1)
    unit_two, inverse_two = norm_parts(ref.first_norm[...] + down + bias_down)
    ref.encoded[...] = (unit_two * gain_second + shift_second).astype(jnp.bfloat16)

    order = [(da, ds, dt) for dt in range(1, side) for ds in list(range(1, side)) + [0] for da in list(range(1, depth)) + [0]]
    order += [(da, ds, 0) for ds in range(1, side) for da in list(range(1, depth)) + [0]]
    order += [(da, 0, 0) for da in list(range(1, depth)) + [0]]

    def number(da, ds, dt):
        return (da * side + ds) * side + dt

    def held_of(w, chip):
        return held[w].at[chip] if w == WEIGHTS else held[w].at[rows_of(w, chip)]

    def scatter_c(w):
        for da, ds, dt in order:
            chip = other.at(da, ds, dt)
            at = number(da, ds, dt)
            send(block(grads[w], w, chip, 1 - core), held_of(w, chip), ref.s_send_c.at[w, at],
                 ref.s_recv_c.at[w, at], sibling)

    def collect(w, da, ds, dt):
        chip = place.at(da, ds, dt)
        arrived(held_of(w, chip), ref.s_recv_c.at[w, number(da, ds, dt)])
        total = block(grads[w], w, chip, core)[...].astype(jnp.float32) + held_of(w, chip)[...].astype(jnp.float32)
        if dt == 0:
            for d in range(1, side):
                at = da * side + ds
                arrived(from_t[w].at[d - 1, at], ref.s_recv_t.at[w, d - 1, at])
                total = total + from_t[w][d - 1, at].astype(jnp.float32)
            if ds == 0:
                for d in range(1, side):
                    arrived(from_s[w].at[d - 1, da], ref.s_recv_s.at[w, d - 1, da])
                    total = total + from_s[w][d - 1, da].astype(jnp.float32)
                if da == 0:
                    for d in range(1, depth):
                        arrived(from_a[w].at[d - 1], ref.s_recv_a.at[w, d - 1])
                        total = total + from_a[w][d - 1].astype(jnp.float32)
        return chip, total

    def relay(w, da, ds, dt, target, ssem, rsem, device):
        chip, total = collect(w, da, ds, dt)
        slot = held_of(w, chip)
        slot[...] = total.astype(held[w].dtype)
        send(slot, target, ssem, rsem, device)

    def scatter_t(w):
        for dt in range(1, side):
            for ds in list(range(1, side)) + [0]:
                for da in list(range(1, depth)) + [0]:
                    at = da * side + ds
                    relay(w, da, ds, dt, from_t[w].at[dt - 1, at], ref.s_send_t.at[w, dt - 1, at],
                          ref.s_recv_t.at[w, dt - 1, at], place.device(0, 0, dt))

    def scatter_s(w):
        for ds in range(1, side):
            for da in list(range(1, depth)) + [0]:
                relay(w, da, ds, 0, from_s[w].at[ds - 1, da], ref.s_send_s.at[w, ds - 1, da],
                      ref.s_recv_s.at[w, ds - 1, da], place.device(0, ds, 0))

    def scatter_a(w):
        for da in range(1, depth):
            relay(w, da, 0, 0, from_a[w].at[da - 1], ref.s_send_a.at[w, da - 1],
                  ref.s_recv_a.at[w, da - 1], place.device(da, 0, 0))

    def finish(w):
        total = collect(w, 0, 0, 0)[1]
        if w == WEIGHTS:
            for j in range(VECTORS):
                out = ref.own_vector[j]
                out[...] = total[j : j + 1, : out.shape[1]]
            return
        mid = total.shape[0] // 2
        ref.final[w][...] = jnp.where(core == 0, total[:mid], total[mid:])
        ref.leave[w][...] = jnp.where(core == 0, total[mid:], total[:mid])
        send(ref.leave[w], ref.enter[w], ref.f_send.at[w], ref.f_recv.at[w], sibling)

    def put_out(w):
        arrived(ref.enter[w], ref.f_recv.at[w])
        mine, theirs = ref.final[w][...], ref.enter[w][...]
        half = mine.shape[1]
        ref.own[w][:, :half] = jnp.where(core == 0, mine, theirs)
        ref.own[w][:, half:] = jnp.where(core == 0, theirs, mine)

    out_grad = ref.out_grad[...].astype(jnp.float32)
    grad_second = norm_back(out_grad, gain_second, unit_two, inverse_two)
    grad_ff = grad_second.astype(jnp.bfloat16)
    ref.grad_ff[...] = grad_ff
    half = weights[3].shape[2]
    for h in range(2):
        for c in range(0, hidden, CHUNK):
            part = dot(ref.active_t[c : c + CHUNK, :], ref.grad_ff[:, h * half : (h + 1) * half])
            grads[3][h, c : c + CHUNK, :] = part.astype(jnp.bfloat16)
    scatter_c(3)
    grad_gain_second = column_sum(out_grad * unit_two)
    grad_shift_second = column_sum(out_grad)
    grad_bias_down = column_sum(grad_ff.astype(jnp.float32))
    ref.grad_second[...] = grad_second
    half_in = weights[2].shape[2]
    bias_parts = []
    for c in range(0, hidden, CHUNK):
        back = dot_nt(ref.grad_ff[:, :half], weights[3][0, c : c + CHUNK, :])
        back = back + dot_nt(ref.grad_ff[:, half:], weights[3][1, c : c + CHUNK, :])
        part = (back * ref.slope[:, c : c + CHUNK]).astype(jnp.bfloat16)
        ref.grad_pre[:, c : c + CHUNK] = part
        bias_parts.append(column_sum(part.astype(jnp.float32)))
    scatter_t(3)
    for h in range(2):
        for c in range(0, half_in, CHUNK):
            at = h * half_in + c
            grads[2][h, :, c : c + CHUNK] = dot(ref.first_t[...], ref.grad_pre[:, at : at + CHUNK]).astype(jnp.bfloat16)
    scatter_c(2)
    grad_first = ref.grad_second[...] + dot_nt(ref.grad_pre[:, :half_in], weights[2][0])
    grad_first = grad_first + dot_nt(ref.grad_pre[:, half_in:], weights[2][1])
    unit_one = ref.unit_one[...]
    grad_first_sum = norm_back(grad_first, gain_first, unit_one, inverse_one)
    ref.grad_first_sum[...] = grad_first_sum
    grad_gain_first = column_sum(grad_first * unit_one)
    grad_shift_first = column_sum(grad_first)
    grad_attn = grad_first_sum.astype(jnp.bfloat16)
    ref.grad_attn[...] = grad_attn
    grad_bias_out = column_sum(grad_attn.astype(jnp.float32))
    scatter_t(2)
    half = weights[1].shape[2]
    for h in range(2):
        grads[1][h] = dot(ref.context_t[...], ref.grad_attn[:, h * half : (h + 1) * half]).astype(jnp.bfloat16)
    scatter_c(1)
    scatter_s(3)
    back = dot_nt(ref.grad_attn[:, :half], weights[1][0]) + dot_nt(ref.grad_attn[:, half:], weights[1][1])
    ref.grad_context[...] = back.astype(jnp.bfloat16)
    for pair in range(heads // 2):
        found = [[], [], []]
        for h in (2 * pair, 2 * pair + 1):
            q, k, v = [qkv[:, i * width + h * HEAD_DIM : i * width + (h + 1) * HEAD_DIM] for i in range(3)]
            grad = ref.grad_context[:, h * HEAD_DIM : (h + 1) * HEAD_DIM]
            weight = ref.attend[h]
            grad_weight = dot_nt(grad, v)
            total = jnp.sum(grad_weight * weight, axis=-1, keepdims=True)
            grad_scores = (weight * (grad_weight - total)).astype(jnp.bfloat16)
            found[0].append(dot(grad_scores, k) * scale)
            found[1].append(dot_tn(grad_scores, q) * scale)
            found[2].append(dot_tn(weight.astype(jnp.bfloat16), grad))
        for i in range(3):
            at = i * width + pair * 2 * HEAD_DIM
            ref.grad_qkv[:, at : at + 2 * HEAD_DIM] = jnp.concatenate(found[i], axis=1).astype(jnp.bfloat16)
    scatter_t(1)
    half = weights[0].shape[2]
    for h in range(2):
        for c in range(0, half, CHUNK):
            at = h * half + c
            grads[0][h, :, c : c + CHUNK] = dot(ref.tokens_t[...], ref.grad_qkv[:, at : at + CHUNK]).astype(jnp.bfloat16)
    scatter_c(0)
    columns = column_sum(ref.grad_qkv[...].astype(jnp.float32))
    found = [columns[:, :width], columns[:, 2 * width :], grad_bias_out, grad_gain_first, grad_shift_first,
             grad_bias_down, grad_gain_second, grad_shift_second]
    found = jnp.concatenate(found + [jnp.zeros_like(grad_bias_out)] * (SMALL_ROWS - len(found)), axis=0)
    mask = owner_mask(devices, SMALL_ROWS, width, piece)
    spread = jnp.where(mask, jnp.concatenate([found] * devices, axis=0), 0.0)
    ninth = jnp.where(owner_mask(devices, 1, hidden, wide), jnp.concatenate(bias_parts, axis=1), 0.0)
    small = jnp.zeros((devices * SMALL_ROWS, LANES), jnp.float32)
    small_in = jnp.zeros((devices, LANES), jnp.float32)
    for _ in range(3):
        low = spread.astype(jnp.bfloat16)
        small = small + dot_nt(low, lane_owner(LANES, width, piece))
        spread = spread - low.astype(jnp.float32)
        low = ninth.astype(jnp.bfloat16)
        small_in = small_in + dot_nt(low, lane_owner(LANES, hidden, wide))
        ninth = ninth - low.astype(jnp.float32)
    row = lax.broadcasted_iota(jnp.int32, (devices, SMALL_ROWS, LANES), 1)
    small = jnp.where(row == VECTORS - 1, small_in.reshape(devices, 1, LANES), small.reshape(devices, SMALL_ROWS, LANES))
    grads[WEIGHTS][...] = small.reshape(chips, 2, SMALL_ROWS, LANES)
    scatter_c(WEIGHTS)
    scatter_s(2)
    scatter_t(0)
    scatter_t(WEIGHTS)
    half = weights[0].shape[2]
    grad_tokens = ref.grad_first_sum[...] + dot_nt(ref.grad_qkv[:, :half], weights[0][0])
    ref.grad_tokens[...] = grad_tokens + dot_nt(ref.grad_qkv[:, half:], weights[0][1])
    scatter_a(3)
    scatter_s(1)
    scatter_a(2)
    scatter_s(0)
    scatter_s(WEIGHTS)
    scatter_a(1)
    scatter_a(0)
    scatter_a(WEIGHTS)
    for w in (3, 2, 1, 0, WEIGHTS):
        finish(w)
    for w in (3, 2, 1, 0):
        put_out(w)
    for copy in started:
        copy.wait_send()


def publish_kernel(*refs):
    for source, target in zip(refs[: len(refs) // 2], refs[len(refs) // 2 :]):
        target[...] = source[...]


def whole_layer(tokens, lengths, matrices, vectors, out_grad, devices):
    rows, width = tokens.shape
    hidden = matrices[2].shape[1]
    chips = devices // 2
    side = max(s for s in range(1, chips + 1) if s**3 <= chips and chips % (s * s) == 0)
    depth = chips // (side * side)
    count = WEIGHTS + 1

    def low(*shape):
        return jax.ShapeDtypeStruct(shape, jnp.bfloat16)

    def full(*shape):
        return jax.ShapeDtypeStruct(shape, jnp.float32)

    def per_block(*lead):
        blocks = [low(*lead, 2 * m.shape[0], m.shape[1] // 2) for m in matrices]
        return blocks + [full(*lead, SMALL_ROWS, LANES)]

    args = dict(
        tokens=tokens, lengths=lengths, out_grad=out_grad, shard=list(matrices),
        vector=[v.reshape(1, -1) for v in vectors])
    outs = dict(
        encoded=low(rows, width), grad_tokens=full(rows, width),
        own=[full(*m.shape) for m in matrices],
        own_vector=[full(1, v.shape[0]) for v in vectors])
    held = [low(m.shape[0] * devices, m.shape[1] // 2) for m in matrices]
    halves = [low(2, *h.shape) for h in held]
    pieces = [full(m.shape[0], m.shape[1] // 2) for m in matrices]
    small = full(chips, 2, SMALL_ROWS, LANES)
    heads = width // HEAD_DIM
    scratch = dict(
        raw=[low(*m.shape) for m in matrices], weight=halves + [small], grad=halves + [small],
        held=held + [full(chips, SMALL_ROWS, LANES)],
        from_t=per_block(side - 1, depth * side), from_s=per_block(side - 1, depth),
        from_a=per_block(depth - 1), final=pieces, leave=pieces, enter=pieces,
        pack=full(SMALL_ROWS, LANES),
        context=low(rows, width), first_low=low(rows, width), grad_ff=low(rows, width),
        grad_attn=low(rows, width), grad_context=low(rows, width),
        tokens_t=low(width, rows), context_t=low(width, rows), first_t=low(width, rows),
        unit_one=full(rows, width), first_norm=full(rows, width),
        grad_second=full(rows, width), grad_first_sum=full(rows, width),
        qkv=low(rows, 3 * width), grad_qkv=low(rows, 3 * width),
        active=low(rows, hidden), grad_pre=low(rows, hidden), active_t=low(hidden, rows),
        slope=full(rows, hidden), attend=full(heads, rows, rows))
    by_a, by_s, by_t = (count, depth - 1), (count, side - 1, depth), (count, side - 1, depth * side)
    by_c, by_w = (count, chips), (WEIGHTS,)
    sems = dict(
        g_send_a=by_a, g_recv_a=by_a, s_send_a=by_a, s_recv_a=by_a,
        g_send_s=by_s, g_recv_s=by_s, s_send_s=by_s, s_recv_s=by_s,
        g_send_t=by_t, g_recv_t=by_t, s_send_t=by_t, s_recv_t=by_t,
        g_send_c=by_c, g_recv_c=by_c, s_send_c=by_c, s_recv_c=by_c,
        raw_send=by_w, raw_recv=by_w, f_send=by_w, f_recv=by_w)
    sems = {name: pltpu.SemaphoreType.DMA(shape) for name, shape in sems.items()}
    vmem = pl.BlockSpec(memory_space=pltpu.VMEM)
    smem = pl.BlockSpec(memory_space=pltpu.SMEM)
    arg_list, arg_tree = jax.tree.flatten(args)
    out_list, out_tree = jax.tree.flatten(outs)
    scratch_list, scratch_tree = jax.tree.flatten(scratch)

    def kernel(*refs):
        cuts = [len(arg_list), len(arg_list) + len(out_list)]
        cuts.append(cuts[1] + len(scratch_list))
        ref = SimpleNamespace(
            **jax.tree.unflatten(arg_tree, refs[: cuts[0]]),
            **jax.tree.unflatten(out_tree, refs[cuts[0] : cuts[1]]),
            **jax.tree.unflatten(scratch_tree, refs[cuts[1] : cuts[2]]),
            **dict(zip(sems, refs[cuts[2] :])))
        layer_kernel(devices, ref)

    found = pl.pallas_call(
        kernel,
        out_shape=out_list,
        in_specs=[smem if a is lengths else vmem for a in arg_list],
        out_specs=[vmem] * len(out_list),
        scratch_shapes=[pltpu.VMEM(s.shape, s.dtype) for s in scratch_list] + list(sems.values()),
        compiler_params=pltpu.CompilerParams(
            collective_id=0, has_side_effects=True, vmem_limit_bytes=VMEM_BYTES),
        name="encoder_layer",
    )(*arg_list)
    found = pl.pallas_call(
        publish_kernel,
        out_shape=out_list,
        in_specs=[vmem] * len(out_list),
        out_specs=[vmem] * len(out_list),
        name="publish",
    )(*found)
    out = SimpleNamespace(**jax.tree.unflatten(out_tree, found))
    own_qkv, own_out, own_in, own_down = out.own
    own = [v.reshape(-1) for v in out.own_vector]
    return (out.encoded, out.grad_tokens, own_qkv, own[0], own[1], own_out, own[2], own[3], own[4],
            own_in, own[8], own_down, own[5], own[6], own[7])


def pack_rows(vectors, blocks, dtype):
    rows = []
    for v in vectors:
        piece = v.astype(dtype).reshape(blocks, 1, -1)
        rows.append(jnp.pad(piece, ((0, 0), (0, 0), (0, LANES - piece.shape[2]))))
    rows.append(jnp.zeros((blocks, SMALL_ROWS - len(vectors), LANES), dtype))
    return jnp.concatenate(rows, axis=1)


def unpack_rows(packed, lengths):
    return [packed[:, j, :n].reshape(-1) for j, n in enumerate(lengths)]


def gather_params(matrices, vectors, devices):
    lengths = [v.shape[0] for v in vectors]
    small = pack_rows(vectors, 1, jnp.bfloat16)[0]
    full = [lax.all_gather(m, "dp", axis=0, tiled=True) for m in matrices]
    small_full = lax.all_gather(small, "dp", axis=0)
    return full, unpack_rows(small_full, lengths)


def scatter_grads(matrices, vectors, devices):
    lengths = [v.shape[0] // devices for v in vectors]
    small = pack_rows(vectors, devices, jnp.float32)
    owned = [lax.psum_scatter(m, "dp", scatter_dimension=0, tiled=True) for m in matrices]
    small_owned = lax.psum_scatter(small, "dp", scatter_dimension=0, tiled=True)[0]
    return owned, [small_owned[j, :n] for j, n in enumerate(lengths)]


def layer_norm(hidden, gain, shift):
    center = jnp.mean(hidden, axis=-1, keepdims=True)
    centered = hidden - center
    spread = jnp.mean(centered * centered, axis=-1, keepdims=True)
    return centered * lax.rsqrt(spread + 1e-06) * gain + shift


def gelu_exact(values):
    return jax.nn.gelu(values, approximate=False)


def to_low(values):
    return values.astype(jnp.bfloat16)


def as_float(values):
    return values.astype(jnp.float32)


def matmul(left, right):
    return jnp.dot(left, right, preferred_element_type=jnp.float32)


def matmul_left_t(left, right):
    return lax.dot_general(
        left, right, (((0,), (0,)), ((), ())), preferred_element_type=jnp.float32
    )


def matmul_right_t(left, right):
    return lax.dot_general(
        left, right, (((1,), (1,)), ((), ())), preferred_element_type=jnp.float32
    )


def masked_scores(queries, keys, allowed):
    raw = jnp.einsum(
        "hqd,hkd->hqk", queries, keys, preferred_element_type=jnp.float32
    ) * HEAD_DIM ** (-0.5)
    return jnp.where(allowed[None], raw, -1e30)


def body(
    tokens,
    lengths,
    qkv_weight,
    query_bias,
    value_bias,
    out_weight,
    out_bias,
    norm_one_gain,
    norm_one_shift,
    ff_in_weight,
    ff_in_bias,
    ff_out_weight,
    ff_out_bias,
    norm_two_gain,
    norm_two_shift,
    out_grad,
):
    rows, width = tokens.shape
    heads = width // HEAD_DIM
    scale = HEAD_DIM ** (-0.5)
    devices = lax.axis_size("dp")
    if qkv_weight.shape[0] % 8 == 0:
        return whole_layer(
            tokens,
            lengths,
            (qkv_weight, out_weight, ff_in_weight, ff_out_weight),
            (
                query_bias,
                value_bias,
                out_bias,
                norm_one_gain,
                norm_one_shift,
                ff_out_bias,
                norm_two_gain,
                norm_two_shift,
                ff_in_bias,
            ),
            out_grad,
            devices,
        )
    (weight_qkv, weight_out, weight_in, weight_down), vectors = gather_params(
        (qkv_weight, out_weight, ff_in_weight, ff_out_weight),
        (
            query_bias,
            value_bias,
            out_bias,
            norm_one_gain,
            norm_one_shift,
            ff_out_bias,
            norm_two_gain,
            norm_two_shift,
            ff_in_bias,
        ),
        devices,
    )
    (bias_query, bias_value, bias_out, gain_first, shift_first, bias_down, gain_second,
     shift_second, bias_in) = vectors
    bounds = jnp.cumsum(lengths)
    position = jnp.arange(rows, dtype=jnp.int32)
    segments = jnp.sum((position[:, None] >= bounds[None, :]).astype(jnp.int32), axis=1)
    allowed = segments[:, None] == segments[None, :]
    zero_keys = jnp.zeros((width,), jnp.float32)
    qkv_bias = jnp.concatenate([as_float(bias_query), zero_keys, as_float(bias_value)])
    projected = to_low(matmul(tokens, weight_qkv) + qkv_bias)
    split = projected.reshape(rows, 3, heads, HEAD_DIM).transpose(1, 2, 0, 3)
    queries, keys, values = (split[0], split[1], split[2])
    scores = masked_scores(queries, keys, allowed)
    peak = jnp.max(scores, axis=-1, keepdims=True)
    log_total = peak + jnp.log(jnp.sum(jnp.exp(scores - peak), axis=-1, keepdims=True))
    attend = jnp.exp(scores - log_total)
    context = jnp.einsum("hqk,hkd->qhd", to_low(attend), values, preferred_element_type=jnp.float32)
    context = to_low(context.reshape(rows, width))
    first_sum = as_float(tokens) + matmul(context, weight_out) + as_float(bias_out)
    first_norm, norm_one_pull = jax.vjp(
        layer_norm, first_sum, as_float(gain_first), as_float(shift_first)
    )
    first_low = to_low(first_norm)
    pre_act = matmul(first_low, weight_in) + as_float(bias_in)
    activated = to_low(gelu_exact(pre_act))
    second_sum = first_norm + matmul(activated, weight_down) + as_float(bias_down)
    encoded, norm_two_pull = jax.vjp(
        layer_norm, second_sum, as_float(gain_second), as_float(shift_second)
    )
    grad_second, grad_gain_second, grad_shift_second = norm_two_pull(as_float(out_grad))
    grad_ff = to_low(grad_second)
    grad_weight_down = matmul_left_t(activated, grad_ff)
    grad_bias_down = jnp.sum(as_float(grad_ff), axis=0)
    grad_act = matmul_right_t(grad_ff, weight_down)
    gelu_pull = jax.vjp(gelu_exact, pre_act)[1]
    grad_pre = to_low(gelu_pull(grad_act)[0])
    grad_weight_in = matmul_left_t(first_low, grad_pre)
    grad_bias_in = jnp.sum(as_float(grad_pre), axis=0)
    grad_first = grad_second + matmul_right_t(grad_pre, weight_in)
    grad_first_sum, grad_gain_first, grad_shift_first = norm_one_pull(grad_first)
    grad_attn = to_low(grad_first_sum)
    grad_weight_out = matmul_left_t(context, grad_attn)
    grad_bias_out = jnp.sum(as_float(grad_attn), axis=0)
    grad_context = to_low(matmul_right_t(grad_attn, weight_out))
    grad_heads = grad_context.reshape(rows, heads, HEAD_DIM).transpose(1, 0, 2)
    again_scores = masked_scores(queries, keys, allowed)
    again_attend = jnp.exp(again_scores - log_total)
    grad_values = jnp.einsum(
        "hqk,hqd->hkd", to_low(again_attend), grad_heads, preferred_element_type=jnp.float32
    )
    grad_attend = jnp.einsum("hqd,hkd->hqk", grad_heads, values, preferred_element_type=jnp.float32)
    row_total = jnp.sum(grad_attend * again_attend, axis=-1, keepdims=True)
    grad_scores = to_low(again_attend * (grad_attend - row_total))
    grad_queries = (
        jnp.einsum("hqk,hkd->hqd", grad_scores, keys, preferred_element_type=jnp.float32) * scale
    )
    grad_keys = (
        jnp.einsum("hqk,hqd->hkd", grad_scores, queries, preferred_element_type=jnp.float32) * scale
    )
    grad_qkv = to_low(
        jnp.stack([grad_queries, grad_keys, grad_values])
        .transpose(2, 0, 1, 3)
        .reshape(rows, 3 * width)
    )
    grad_weight_qkv = matmul_left_t(tokens, grad_qkv)
    grad_columns = jnp.sum(as_float(grad_qkv), axis=0)
    grad_bias_query = grad_columns[:width]
    grad_bias_value = grad_columns[2 * width :]
    grad_tokens = grad_first_sum + matmul_right_t(grad_qkv, weight_qkv)
    (own_down, own_in, own_out, own_qkv), own = scatter_grads(
        (grad_weight_down, grad_weight_in, grad_weight_out, grad_weight_qkv),
        (
            grad_bias_query,
            grad_bias_value,
            grad_bias_out,
            grad_gain_first,
            grad_shift_first,
            grad_bias_down,
            grad_gain_second,
            grad_shift_second,
            grad_bias_in,
        ),
        devices,
    )
    return (
        to_low(encoded),
        grad_tokens,
        own_qkv,
        own[0],
        own[1],
        own_out,
        own[2],
        own[3],
        own[4],
        own_in,
        own[8],
        own_down,
        own[5],
        own[6],
        own[7],
    )


def solution(mesh):
    in_specs = (
        P("dp", None),
        P("dp"),
        P("dp", None),
        P("dp"),
        P("dp"),
        P("dp", None),
        P("dp"),
        P("dp"),
        P("dp"),
        P("dp", None),
        P("dp"),
        P("dp", None),
        P("dp"),
        P("dp"),
        P("dp"),
        P("dp", None),
    )
    out_specs = (
        P("dp", None),
        P("dp", None),
        P("dp", None),
        P("dp"),
        P("dp"),
        P("dp", None),
        P("dp"),
        P("dp"),
        P("dp"),
        P("dp", None),
        P("dp"),
        P("dp", None),
        P("dp"),
        P("dp"),
        P("dp"),
    )
    return jax.shard_map(body, mesh=mesh, in_specs=in_specs, out_specs=out_specs, check_vma=False)
```

```python
from types import SimpleNamespace

import jax
import jax.numpy as jnp
from jax import lax
from jax.experimental import pallas as pl
from jax.experimental.pallas import tpu as pltpu
from jax.sharding import PartitionSpec as P

HEAD_DIM = 64
SMALL_ROWS = 16
LANES = 128
VMEM_BYTES = 60 * 1024 * 1024
MESH = pl.DeviceIdType.MESH


class Place:
    def __init__(self, devices, core=None):
        self.chips = devices // 2
        side = max(s for s in range(1, self.chips + 1) if s**3 <= self.chips and self.chips % (s * s) == 0)
        self.side = side
        self.depth = self.chips // (side * side)
        me = lax.axis_index("dp")
        self.chip = me // 2
        self.own_core = lax.rem(me, 2)
        self.core = self.own_core if core is None else core(self.own_core)
        first = self.core == 0
        self.step_a = side * side
        self.step_s = jnp.where(first, side, 1)
        self.step_t = jnp.where(first, 1, side)
        self.pos_a = self.chip // self.step_a
        mid = lax.rem(self.chip // side, side)
        low = lax.rem(self.chip, side)
        self.pos_s = jnp.where(first, mid, low)
        self.pos_t = jnp.where(first, low, mid)

    def at(self, da, ds, dt):
        a = lax.rem(self.pos_a + da, self.depth)
        s = lax.rem(self.pos_s + ds, self.side)
        t = lax.rem(self.pos_t + dt, self.side)
        return a * self.step_a + s * self.step_s + t * self.step_t

    def device(self, da, ds, dt):
        return self.at(da, ds, dt) * 2 + self.own_core

    def sibling(self):
        return self.chip * 2 + 1 - self.own_core

    def peers(self):
        found = [self.sibling()]
        found += [self.device(d, 0, 0) for d in range(1, self.depth)]
        found += [self.device(0, d, 0) for d in range(1, self.side)]
        found += [self.device(0, 0, d) for d in range(1, self.side)]
        return found


def greet(place):
    barrier = pltpu.get_barrier_semaphore()
    peers = place.peers()
    for peer in peers:
        pl.semaphore_signal(barrier, inc=1, device_id=(peer,), device_id_type=MESH)
    pl.semaphore_wait(barrier, len(peers))


WEIGHTS = 4
VECTORS = 9
TURNED = (3,)
CHUNK = 384


def dot(left, right):
    return jnp.dot(left, right, preferred_element_type=jnp.float32)


def dot_nt(left, right):
    return lax.dot_general(left, right, (((1,), (1,)), ((), ())), preferred_element_type=jnp.float32)


def dot_tn(left, right):
    return lax.dot_general(left, right, (((0,), (0,)), ((), ())), preferred_element_type=jnp.float32)


def erf_rational(x):
    x = jnp.clip(x, -3.832506856900711, 3.832506856900711)
    y = x * x
    top = jnp.full_like(y, 0.00022905065861350646)
    for c in (0.0034082910107109506, 0.050955695062380861, 0.18520832239976145, 1.128379143519084):
        top = top * y + c
    low = jnp.full_like(y, -1.1791602954361697e-7)
    for c in (0.000023547966471313185, 0.0010179625278914885, 0.014070470171167667,
              0.11098505178285362, 0.49746925110067538, 1.0):
        low = low * y + c
    return x * top / low


def norm_parts(hidden):
    center = jnp.mean(hidden, axis=-1, keepdims=True)
    centered = hidden - center
    inverse = lax.rsqrt(jnp.mean(centered * centered, axis=-1, keepdims=True) + 1e-06)
    return centered * inverse, inverse


def norm_back(grad, gain, unit, inverse):
    scaled = grad * gain
    mean_one = jnp.mean(scaled, axis=-1, keepdims=True)
    mean_two = jnp.mean(scaled * unit, axis=-1, keepdims=True)
    return inverse * (scaled - mean_one - unit * mean_two)


def column_sum(values):
    return jnp.sum(values, axis=0, keepdims=True)


def lane_owner(rows, columns, piece):
    row = lax.broadcasted_iota(jnp.int32, (rows, columns), 0)
    column = lax.broadcasted_iota(jnp.int32, (rows, columns), 1)
    return (lax.rem(column, piece) == row).astype(jnp.bfloat16)


def owner_mask(devices, repeat, columns, piece):
    row = lax.broadcasted_iota(jnp.int32, (devices * repeat, columns), 0)
    column = lax.broadcasted_iota(jnp.int32, (devices * repeat, columns), 1)
    start = (row // repeat) * piece
    return jnp.logical_and(column >= start, column < start + piece)


def layer_kernel(devices, ref):
    place = Place(devices)
    other = Place(devices, lambda own_core: 1 - own_core)
    depth, side, core = place.depth, place.side, place.core
    chips = devices // 2
    sibling = place.sibling()
    count = WEIGHTS + 1
    weights = ref.weight
    grads = ref.grad
    held = ref.held
    from_t = ref.from_t
    from_s = ref.from_s
    from_a = ref.from_a
    shards = ref.shard
    raws = ref.raw
    started = []

    def send(source, target, ssem, rsem, device):
        copy = pltpu.make_async_remote_copy(
            src_ref=source, dst_ref=target, send_sem=ssem, recv_sem=rsem,
            device_id=(device,), device_id_type=MESH)
        copy.start()
        started.append(copy)

    def arrived(target, rsem):
        pltpu.make_async_remote_copy(
            src_ref=target, dst_ref=target, send_sem=rsem, recv_sem=rsem,
            device_id=(sibling,), device_id_type=MESH).wait_recv()

    def rows_of(w, chip):
        rows = 2 * shards[w].shape[0]
        return pl.ds(pl.multiple_of(chip * rows, rows), rows)

    def block(array, w, chip, of_core):
        if w == WEIGHTS:
            return array.at[chip, of_core]
        return array.at[of_core, rows_of(w, chip)]

    own = place.at(0, 0, 0)
    piece = ref.vector[0].shape[1]
    wide = ref.vector[8].shape[1]
    pack = ref.pack
    pack[...] = jnp.zeros_like(pack)
    for j in range(VECTORS):
        v = ref.vector[j]
        pack[j : j + 1, 0 : v.shape[1]] = v[...].astype(jnp.float32)
    weights[WEIGHTS][own, core] = pack[...]
    for w in range(WEIGHTS):
        send(shards[w], raws[w], ref.raw_send.at[w], ref.raw_recv.at[w], sibling)

    def pass_on(w, chip, da, ds, dt, to_a, to_s, to_t):
        part = block(weights[w], w, chip, core)
        if to_a:
            for d in range(1, depth):
                send(part, part, ref.g_send_a.at[w, d - 1, ds], ref.g_recv_a.at[w, d - 1, ds], place.device(d, 0, 0))
        if to_s:
            for d in range(1, side):
                send(part, part, ref.g_send_s.at[w, d - 1, da], ref.g_recv_s.at[w, d - 1, da], place.device(0, d, 0))
        if to_t:
            for d in range(1, side):
                at = da * side + ds
                send(part, part, ref.g_send_t.at[w, d - 1, at], ref.g_recv_t.at[w, d - 1, at], place.device(0, 0, d))
        if (da, ds, dt) != (0, 0, 0) or w == WEIGHTS:
            at = (da * side + ds) * side + dt
            send(part, part, ref.g_send_c.at[w, at], ref.g_recv_c.at[w, at], sibling)

    def gather_own(w):
        if w < WEIGHTS:
            arrived(raws[w], ref.raw_recv.at[w])
            mine = shards[w][...].astype(jnp.float32)
            theirs = raws[w][...].astype(jnp.float32)
            both = jnp.concatenate(
                [jnp.where(core == 0, mine, theirs), jnp.where(core == 0, theirs, mine)], axis=0).astype(jnp.bfloat16)
            half = both.shape[1] // 2
            weights[w][0, rows_of(w, own)] = both[:, :half]
            weights[w][1, rows_of(w, own)] = both[:, half:]
        pass_on(w, own, 0, 0, 0, True, True, True)

    def gather_a(w):
        for da in range(1, depth):
            for ds in range(side if w in TURNED else 1):
                chip = place.at(depth - da, (side - ds) % side, 0)
                arrived(block(weights[w], w, chip, core), ref.g_recv_a.at[w, da - 1, ds])
                pass_on(w, chip, da, ds, 0, False, w not in TURNED, True)

    def gather_s(w):
        for da in range(1 if w in TURNED else depth):
            for ds in range(1, side):
                chip = place.at((depth - da) % depth, side - ds, 0)
                arrived(block(weights[w], w, chip, core), ref.g_recv_s.at[w, ds - 1, da])
                pass_on(w, chip, da, ds, 0, w in TURNED, False, True)

    def gather_t(w):
        for da in range(depth):
            for ds in range(side):
                for dt in range(1, side):
                    chip = place.at((depth - da) % depth, (side - ds) % side, side - dt)
                    arrived(block(weights[w], w, chip, core), ref.g_recv_t.at[w, dt - 1, da * side + ds])
                    pass_on(w, chip, da, ds, dt, False, False, False)

    def gather_c(w):
        for da in range(depth):
            for ds in range(side):
                for dt in range(side):
                    if (da, ds, dt) == (0, 0, 0) and w < WEIGHTS:
                        continue
                    chip = other.at((depth - da) % depth, (side - ds) % side, (side - dt) % side)
                    arrived(block(weights[w], w, chip, 1 - core),
                            ref.g_recv_c.at[w, (da * side + ds) * side + dt])

    for w in (WEIGHTS, 0, 1, 2, 3):
        gather_own(w)
    gather_a(WEIGHTS)
    gather_a(0)
    gather_s(3)
    gather_a(1)
    gather_s(WEIGHTS)
    gather_s(0)
    gather_a(2)
    gather_s(1)

    tokens = ref.tokens
    rows, width = tokens.shape
    hidden = weights[2].shape[2] * 2
    heads = width // HEAD_DIM
    scale = HEAD_DIM ** (-0.5)
    qkv, context = ref.qkv, ref.context
    ref.tokens_t[...] = tokens[...].T
    position_r = lax.broadcasted_iota(jnp.int32, (rows, rows), 0)
    position_c = lax.broadcasted_iota(jnp.int32, (rows, rows), 1)
    segment_r = jnp.zeros((rows, rows), jnp.int32)
    segment_c = jnp.zeros((rows, rows), jnp.int32)
    bound = jnp.int32(0)
    for slot in range(ref.lengths.shape[0]):
        bound = bound + ref.lengths[slot]
        segment_r = segment_r + (position_r >= bound).astype(jnp.int32)
        segment_c = segment_c + (position_c >= bound).astype(jnp.int32)
    allowed = segment_r == segment_c

    gather_t(WEIGHTS)
    gather_c(WEIGHTS)
    packed = weights[WEIGHTS][...].reshape(devices * SMALL_ROWS, LANES)
    spread = dot(packed.astype(jnp.bfloat16), lane_owner(LANES, width, piece))
    spread = jnp.where(owner_mask(devices, SMALL_ROWS, width, piece), spread, 0.0)
    pick = lane_owner(SMALL_ROWS, devices * SMALL_ROWS, SMALL_ROWS)
    vectors = dot(pick, spread.astype(jnp.bfloat16))
    ninth = dot(weights[WEIGHTS][...].reshape(devices, SMALL_ROWS, LANES)[:, VECTORS - 1, :].astype(jnp.bfloat16),
                lane_owner(LANES, hidden, wide))
    bias_in = column_sum(jnp.where(owner_mask(devices, 1, hidden, wide), ninth, 0.0))
    bias_query, bias_value, bias_out, gain_first, shift_first, bias_down, gain_second, shift_second = [
        vectors[j : j + 1] for j in range(8)]
    qkv_bias = jnp.concatenate([bias_query, jnp.zeros_like(bias_query), bias_value], axis=1)

    gather_t(0)
    gather_c(0)
    half = weights[0].shape[2]
    for h in range(2):
        for c in range(0, half, CHUNK):
            at = h * half + c
            out = dot(tokens[...], weights[0][h, :, c : c + CHUNK]) + qkv_bias[:, at : at + CHUNK]
            qkv[:, at : at + CHUNK] = out.astype(jnp.bfloat16)
    gather_s(2)
    for pair in range(heads // 2):
        found = []
        for h in (2 * pair, 2 * pair + 1):
            q, k, v = [qkv[:, i * width + h * HEAD_DIM : i * width + (h + 1) * HEAD_DIM] for i in range(3)]
            scores = jnp.where(allowed, dot_nt(q, k) * scale, -1e30)
            weight = jnp.exp(scores - jnp.max(scores, axis=-1, keepdims=True))
            weight = weight / jnp.sum(weight, axis=-1, keepdims=True)
            ref.attend[h] = weight
            found.append(dot(weight.astype(jnp.bfloat16), v))
        at = pair * 2 * HEAD_DIM
        context[:, at : at + 2 * HEAD_DIM] = jnp.concatenate(found, axis=1).astype(jnp.bfloat16)
    gather_a(3)
    ref.context_t[...] = context[...].T

    gather_t(1)
    gather_t(2)
    gather_c(1)
    attn = jnp.concatenate([dot(context[...], weights[1][h]) for h in range(2)], axis=1)
    unit_one, inverse_one = norm_parts(tokens[...].astype(jnp.float32) + attn + bias_out)
    ref.unit_one[...] = unit_one
    first_norm = unit_one * gain_first + shift_first
    ref.first_norm[...] = first_norm
    first_low = first_norm.astype(jnp.bfloat16)
    ref.first_low[...] = first_low
    ref.first_t[...] = first_low.T
    gather_t(3)
    gather_c(2)
    half = weights[2].shape[2]
    for h in range(2):
        for c in range(0, half, CHUNK):
            at = h * half + c
            pre = dot(ref.first_low[...], weights[2][h, :, c : c + CHUNK]) + bias_in[:, at : at + CHUNK]
            gate = 0.5 + 0.5 * erf_rational(pre * (0.5**0.5))
            act = (pre * gate).astype(jnp.bfloat16)
            ref.active[:, at : at + CHUNK] = act
            ref.active_t[at : at + CHUNK, :] = act.T
            ref.slope[:, at : at + CHUNK] = gate + pre * (0.3989422804014327 * jnp.exp(-0.5 * pre * pre))
    gather_c(3)
    down = jnp.concatenate([dot(ref.active[...], weights[3][h]) for h in range(2)], axis=1)
    unit_two, inverse_two = norm_parts(ref.first_norm[...] + down + bias_down)
    ref.encoded[...] = (unit_two * gain_second + shift_second).astype(jnp.bfloat16)
    ref.ship(0)

    order = [(da, ds, dt) for dt in range(1, side) for ds in list(range(1, side)) + [0] for da in list(range(1, depth)) + [0]]
    order += [(da, ds, 0) for ds in range(1, side) for da in list(range(1, depth)) + [0]]
    order += [(da, 0, 0) for da in list(range(1, depth)) + [0]]

    def number(da, ds, dt):
        return (da * side + ds) * side + dt

    def held_of(w, chip):
        return held[w].at[chip] if w == WEIGHTS else held[w].at[rows_of(w, chip)]

    def scatter_c(w):
        for da, ds, dt in order:
            chip = other.at(da, ds, dt)
            at = number(da, ds, dt)
            send(block(grads[w], w, chip, 1 - core), held_of(w, chip), ref.s_send_c.at[w, at],
                 ref.s_recv_c.at[w, at], sibling)

    def collect(w, da, ds, dt):
        chip = place.at(da, ds, dt)
        arrived(held_of(w, chip), ref.s_recv_c.at[w, number(da, ds, dt)])
        total = block(grads[w], w, chip, core)[...].astype(jnp.float32) + held_of(w, chip)[...].astype(jnp.float32)
        if dt == 0:
            for d in range(1, side):
                at = da * side + ds
                arrived(from_t[w].at[d - 1, at], ref.s_recv_t.at[w, d - 1, at])
                total = total + from_t[w][d - 1, at].astype(jnp.float32)
            if ds == 0 and (da == 0 or w not in TURNED):
                for d in range(1, side):
                    arrived(from_s[w].at[d - 1, da], ref.s_recv_s.at[w, d - 1, da])
                    total = total + from_s[w][d - 1, da].astype(jnp.float32)
            if da == 0 and (ds == 0 or w in TURNED):
                for d in range(1, depth):
                    arrived(from_a[w].at[d - 1, ds], ref.s_recv_a.at[w, d - 1, ds])
                    total = total + from_a[w][d - 1, ds].astype(jnp.float32)
        return chip, total

    def relay(w, da, ds, dt, target, ssem, rsem, device):
        chip, total = collect(w, da, ds, dt)
        slot = held_of(w, chip)
        slot[...] = total.astype(held[w].dtype)
        send(slot, target, ssem, rsem, device)

    def scatter_t(w):
        lines = [(da, ds) for ds in list(range(1, side)) + [0] for da in list(range(1, depth)) + [0]]
        if w in TURNED:
            lines = [(da, ds) for da in list(range(1, depth)) + [0] for ds in list(range(1, side)) + [0]]
        for dt in range(1, side):
            for da, ds in lines:
                at = da * side + ds
                relay(w, da, ds, dt, from_t[w].at[dt - 1, at], ref.s_send_t.at[w, dt - 1, at],
                      ref.s_recv_t.at[w, dt - 1, at], place.device(0, 0, dt))

    def scatter_s(w):
        for ds in range(1, side):
            for da in [0] if w in TURNED else list(range(1, depth)) + [0]:
                relay(w, da, ds, 0, from_s[w].at[ds - 1, da], ref.s_send_s.at[w, ds - 1, da],
                      ref.s_recv_s.at[w, ds - 1, da], place.device(0, ds, 0))

    def scatter_a(w, steps=None):
        for da in steps or range(1, depth):
            for ds in list(range(1, side)) + [0] if w in TURNED else [0]:
                relay(w, da, ds, 0, from_a[w].at[da - 1, ds], ref.s_send_a.at[w, da - 1, ds],
                      ref.s_recv_a.at[w, da - 1, ds], place.device(da, 0, 0))

    def finish(w):
        total = collect(w, 0, 0, 0)[1]
        if w == WEIGHTS:
            for j in range(VECTORS):
                out = ref.own_vector[j]
                out[...] = total[j : j + 1, : out.shape[1]]
            return
        mid = total.shape[0] // 2
        ref.final[w][...] = jnp.where(core == 0, total[:mid], total[mid:])
        ref.leave[w][...] = jnp.where(core == 0, total[mid:], total[:mid])
        send(ref.leave[w], ref.enter[w], ref.f_send.at[w], ref.f_recv.at[w], sibling)

    def put_out(w):
        arrived(ref.enter[w], ref.f_recv.at[w])
        mine, theirs = ref.final[w][...], ref.enter[w][...]
        half = mine.shape[1]
        ref.own[w][:, :half] = jnp.where(core == 0, mine, theirs)
        ref.own[w][:, half:] = jnp.where(core == 0, theirs, mine)

    out_grad = ref.out_grad[...].astype(jnp.float32)
    grad_second = norm_back(out_grad, gain_second, unit_two, inverse_two)
    grad_ff = grad_second.astype(jnp.bfloat16)
    ref.grad_ff[...] = grad_ff
    half = weights[3].shape[2]
    for h in range(2):
        for c in range(0, hidden, CHUNK):
            part = dot(ref.active_t[c : c + CHUNK, :], ref.grad_ff[:, h * half : (h + 1) * half])
            grads[3][h, c : c + CHUNK, :] = part.astype(jnp.bfloat16)
    scatter_c(3)
    grad_gain_second = column_sum(out_grad * unit_two)
    grad_shift_second = column_sum(out_grad)
    grad_bias_down = column_sum(grad_ff.astype(jnp.float32))
    ref.grad_second[...] = grad_second
    half_in = weights[2].shape[2]
    bias_parts = []
    for c in range(0, hidden, CHUNK):
        back = dot_nt(ref.grad_ff[:, :half], weights[3][0, c : c + CHUNK, :])
        back = back + dot_nt(ref.grad_ff[:, half:], weights[3][1, c : c + CHUNK, :])
        part = (back * ref.slope[:, c : c + CHUNK]).astype(jnp.bfloat16)
        ref.grad_pre[:, c : c + CHUNK] = part
        bias_parts.append(column_sum(part.astype(jnp.float32)))
    scatter_t(3)
    for h in range(2):
        for c in range(0, half_in, CHUNK):
            at = h * half_in + c
            grads[2][h, :, c : c + CHUNK] = dot(ref.first_t[...], ref.grad_pre[:, at : at + CHUNK]).astype(jnp.bfloat16)
    scatter_c(2)
    scatter_a(3, range(1, 2))
    grad_first = ref.grad_second[...] + dot_nt(ref.grad_pre[:, :half_in], weights[2][0])
    grad_first = grad_first + dot_nt(ref.grad_pre[:, half_in:], weights[2][1])
    unit_one = ref.unit_one[...]
    grad_first_sum = norm_back(grad_first, gain_first, unit_one, inverse_one)
    ref.grad_first_sum[...] = grad_first_sum
    grad_gain_first = column_sum(grad_first * unit_one)
    grad_shift_first = column_sum(grad_first)
    grad_attn = grad_first_sum.astype(jnp.bfloat16)
    ref.grad_attn[...] = grad_attn
    grad_bias_out = column_sum(grad_attn.astype(jnp.float32))
    scatter_t(2)
    scatter_a(3, range(2, depth))
    half = weights[1].shape[2]
    for h in range(2):
        grads[1][h] = dot(ref.context_t[...], ref.grad_attn[:, h * half : (h + 1) * half]).astype(jnp.bfloat16)
    scatter_c(1)
    back = dot_nt(ref.grad_attn[:, :half], weights[1][0]) + dot_nt(ref.grad_attn[:, half:], weights[1][1])
    ref.grad_context[...] = back.astype(jnp.bfloat16)
    for pair in range(heads // 2):
        found = [[], [], []]
        for h in (2 * pair, 2 * pair + 1):
            q, k, v = [qkv[:, i * width + h * HEAD_DIM : i * width + (h + 1) * HEAD_DIM] for i in range(3)]
            grad = ref.grad_context[:, h * HEAD_DIM : (h + 1) * HEAD_DIM]
            weight = ref.attend[h]
            grad_weight = dot_nt(grad, v)
            total = jnp.sum(grad_weight * weight, axis=-1, keepdims=True)
            grad_scores = (weight * (grad_weight - total)).astype(jnp.bfloat16)
            found[0].append(dot(grad_scores, k) * scale)
            found[1].append(dot_tn(grad_scores, q) * scale)
            found[2].append(dot_tn(weight.astype(jnp.bfloat16), grad))
        for i in range(3):
            at = i * width + pair * 2 * HEAD_DIM
            ref.grad_qkv[:, at : at + 2 * HEAD_DIM] = jnp.concatenate(found[i], axis=1).astype(jnp.bfloat16)
    scatter_t(1)
    half = weights[0].shape[2]
    for h in range(2):
        for c in range(0, half, CHUNK):
            at = h * half + c
            grads[0][h, :, c : c + CHUNK] = dot(ref.tokens_t[...], ref.grad_qkv[:, at : at + CHUNK]).astype(jnp.bfloat16)
    scatter_c(0)
    columns = column_sum(ref.grad_qkv[...].astype(jnp.float32))
    found = [columns[:, :width], columns[:, 2 * width :], grad_bias_out, grad_gain_first, grad_shift_first,
             grad_bias_down, grad_gain_second, grad_shift_second]
    found = jnp.concatenate(found + [jnp.zeros_like(grad_bias_out)] * (SMALL_ROWS - len(found)), axis=0)
    mask = owner_mask(devices, SMALL_ROWS, width, piece)
    spread = jnp.where(mask, jnp.concatenate([found] * devices, axis=0), 0.0)
    ninth = jnp.where(owner_mask(devices, 1, hidden, wide), jnp.concatenate(bias_parts, axis=1), 0.0)
    small = jnp.zeros((devices * SMALL_ROWS, LANES), jnp.float32)
    small_in = jnp.zeros((devices, LANES), jnp.float32)
    for _ in range(3):
        low = spread.astype(jnp.bfloat16)
        small = small + dot_nt(low, lane_owner(LANES, width, piece))
        spread = spread - low.astype(jnp.float32)
        low = ninth.astype(jnp.bfloat16)
        small_in = small_in + dot_nt(low, lane_owner(LANES, hidden, wide))
        ninth = ninth - low.astype(jnp.float32)
    row = lax.broadcasted_iota(jnp.int32, (devices, SMALL_ROWS, LANES), 1)
    small = jnp.where(row == VECTORS - 1, small_in.reshape(devices, 1, LANES), small.reshape(devices, SMALL_ROWS, LANES))
    grads[WEIGHTS][...] = small.reshape(chips, 2, SMALL_ROWS, LANES)
    scatter_c(WEIGHTS)
    scatter_t(0)
    scatter_t(WEIGHTS)
    scatter_s(2)
    half = weights[0].shape[2]
    grad_tokens = ref.grad_first_sum[...] + dot_nt(ref.grad_qkv[:, :half], weights[0][0])
    ref.grad_tokens[...] = grad_tokens + dot_nt(ref.grad_qkv[:, half:], weights[0][1])
    ref.ship(1)
    scatter_a(2)
    scatter_s(1)
    scatter_a(1)
    scatter_s(3)
    scatter_s(0)
    scatter_s(WEIGHTS)
    scatter_a(0)
    scatter_a(WEIGHTS)
    for w in (3, 2, 1, 0, WEIGHTS):
        finish(w)
    for j in range(VECTORS):
        ref.ship(2 + WEIGHTS + j)
    for w in (3, 2, 1, 0):
        put_out(w)
        ref.ship(2 + w)
    for copy in started:
        copy.wait_send()


def publish_kernel(*refs):
    for source, target in zip(refs[: len(refs) // 2], refs[len(refs) // 2 :]):
        target[...] = source[...]


def whole_layer(tokens, lengths, matrices, vectors, out_grad, devices):
    rows, width = tokens.shape
    hidden = matrices[2].shape[1]
    chips = devices // 2
    side = max(s for s in range(1, chips + 1) if s**3 <= chips and chips % (s * s) == 0)
    depth = chips // (side * side)
    count = WEIGHTS + 1

    def low(*shape):
        return jax.ShapeDtypeStruct(shape, jnp.bfloat16)

    def full(*shape):
        return jax.ShapeDtypeStruct(shape, jnp.float32)

    def per_block(*lead):
        blocks = [low(*lead, 2 * m.shape[0], m.shape[1] // 2) for m in matrices]
        return blocks + [full(*lead, SMALL_ROWS, LANES)]

    args = dict(
        tokens=tokens, lengths=lengths, out_grad=out_grad, shard=list(matrices),
        vector=[v.reshape(1, -1) for v in vectors])
    outs = dict(
        encoded=low(rows, width), grad_tokens=full(rows, width),
        own=[full(*m.shape) for m in matrices],
        own_vector=[full(1, v.shape[0]) for v in vectors])
    held = [low(m.shape[0] * devices, m.shape[1] // 2) for m in matrices]
    halves = [low(2, *h.shape) for h in held]
    pieces = [full(m.shape[0], m.shape[1] // 2) for m in matrices]
    small = full(chips, 2, SMALL_ROWS, LANES)
    heads = width // HEAD_DIM
    scratch = dict(
        raw=[low(*m.shape) for m in matrices], weight=halves + [small], grad=halves + [small],
        held=held + [full(chips, SMALL_ROWS, LANES)],
        from_t=per_block(side - 1, depth * side), from_s=per_block(side - 1, depth),
        from_a=per_block(depth - 1, side), final=pieces, leave=pieces, enter=pieces,
        pack=full(SMALL_ROWS, LANES),
        context=low(rows, width), first_low=low(rows, width), grad_ff=low(rows, width),
        grad_attn=low(rows, width), grad_context=low(rows, width),
        tokens_t=low(width, rows), context_t=low(width, rows), first_t=low(width, rows),
        unit_one=full(rows, width), first_norm=full(rows, width),
        grad_second=full(rows, width), grad_first_sum=full(rows, width),
        qkv=low(rows, 3 * width), grad_qkv=low(rows, 3 * width),
        active=low(rows, hidden), grad_pre=low(rows, hidden), active_t=low(hidden, rows),
        slope=full(rows, hidden), attend=full(heads, rows, rows))
    by_a, by_s, by_t = (count, depth - 1, side), (count, side - 1, depth), (count, side - 1, depth * side)
    by_c, by_w = (count, chips), (WEIGHTS,)
    sems = dict(
        g_send_a=by_a, g_recv_a=by_a, s_send_a=by_a, s_recv_a=by_a,
        g_send_s=by_s, g_recv_s=by_s, s_send_s=by_s, s_recv_s=by_s,
        g_send_t=by_t, g_recv_t=by_t, s_send_t=by_t, s_recv_t=by_t,
        g_send_c=by_c, g_recv_c=by_c, s_send_c=by_c, s_recv_c=by_c,
        raw_send=by_w, raw_recv=by_w, f_send=by_w, f_recv=by_w)
    sems = {name: pltpu.SemaphoreType.DMA(shape) for name, shape in sems.items()}
    vmem = pl.BlockSpec(memory_space=pltpu.VMEM)
    anywhere = pl.BlockSpec(memory_space=pl.ANY)
    smem = pl.BlockSpec(memory_space=pltpu.SMEM)
    arg_list, arg_tree = jax.tree.flatten(args)
    out_list, out_tree = jax.tree.flatten(outs)
    scratch_list, scratch_tree = jax.tree.flatten(scratch)

    def kernel(*refs):
        cuts = [len(arg_list), len(arg_list) + len(out_list)]
        cuts.append(cuts[1] + len(scratch_list))
        cuts += [cuts[2] + len(arg_list), cuts[2] + len(arg_list) + len(out_list)]
        in_sems, out_sems = refs[-2:]
        taken = list(refs[: cuts[0]])
        loads = []
        for i, source in enumerate(refs[: cuts[0]]):
            if arg_list[i] is not lengths:
                taken[i] = refs[cuts[2] + i]
                loads.append(pltpu.make_async_copy(source, taken[i], in_sems.at[i]))
                loads[-1].start()
        made = refs[cuts[3] : cuts[4]]
        leaving = []

        def ship(i):
            leaving.append(pltpu.make_async_copy(made[i], refs[cuts[0] + i], out_sems.at[i]))
            leaving[-1].start()

        ref = SimpleNamespace(
            **jax.tree.unflatten(arg_tree, taken),
            **jax.tree.unflatten(out_tree, made),
            **jax.tree.unflatten(scratch_tree, refs[cuts[1] : cuts[2]]),
            **dict(zip(sems, refs[cuts[4] : -2])), ship=ship)
        greet(Place(devices))
        for load in loads:
            load.wait()
        layer_kernel(devices, ref)
        for copy in leaving:
            copy.wait()

    found = pl.pallas_call(
        kernel,
        out_shape=out_list,
        in_specs=[smem if a is lengths else anywhere for a in arg_list],
        out_specs=[anywhere] * len(out_list),
        scratch_shapes=[pltpu.VMEM(s.shape, s.dtype) for s in [*scratch_list, *arg_list, *out_list]]
        + list(sems.values()) + [pltpu.SemaphoreType.DMA((len(arg_list),)), pltpu.SemaphoreType.DMA((len(out_list),))],
        compiler_params=pltpu.CompilerParams(
            collective_id=0, has_side_effects=True, vmem_limit_bytes=VMEM_BYTES),
        name="encoder_layer",
    )(*arg_list)
    found = pl.pallas_call(
        publish_kernel,
        out_shape=out_list,
        in_specs=[vmem] * len(out_list),
        out_specs=[vmem] * len(out_list),
        name="publish",
    )(*found)
    out = SimpleNamespace(**jax.tree.unflatten(out_tree, found))
    own_qkv, own_out, own_in, own_down = out.own
    own = [v.reshape(-1) for v in out.own_vector]
    return (out.encoded, out.grad_tokens, own_qkv, own[0], own[1], own_out, own[2], own[3], own[4],
            own_in, own[8], own_down, own[5], own[6], own[7])


def pack_rows(vectors, blocks, dtype):
    rows = []
    for v in vectors:
        piece = v.astype(dtype).reshape(blocks, 1, -1)
        rows.append(jnp.pad(piece, ((0, 0), (0, 0), (0, LANES - piece.shape[2]))))
    rows.append(jnp.zeros((blocks, SMALL_ROWS - len(vectors), LANES), dtype))
    return jnp.concatenate(rows, axis=1)


def unpack_rows(packed, lengths):
    return [packed[:, j, :n].reshape(-1) for j, n in enumerate(lengths)]


def gather_params(matrices, vectors, devices):
    lengths = [v.shape[0] for v in vectors]
    small = pack_rows(vectors, 1, jnp.bfloat16)[0]
    full = [lax.all_gather(m, "dp", axis=0, tiled=True) for m in matrices]
    small_full = lax.all_gather(small, "dp", axis=0)
    return full, unpack_rows(small_full, lengths)


def scatter_grads(matrices, vectors, devices):
    lengths = [v.shape[0] // devices for v in vectors]
    small = pack_rows(vectors, devices, jnp.float32)
    owned = [lax.psum_scatter(m, "dp", scatter_dimension=0, tiled=True) for m in matrices]
    small_owned = lax.psum_scatter(small, "dp", scatter_dimension=0, tiled=True)[0]
    return owned, [small_owned[j, :n] for j, n in enumerate(lengths)]


def layer_norm(hidden, gain, shift):
    center = jnp.mean(hidden, axis=-1, keepdims=True)
    centered = hidden - center
    spread = jnp.mean(centered * centered, axis=-1, keepdims=True)
    return centered * lax.rsqrt(spread + 1e-06) * gain + shift


def gelu_exact(values):
    return jax.nn.gelu(values, approximate=False)


def to_low(values):
    return values.astype(jnp.bfloat16)


def as_float(values):
    return values.astype(jnp.float32)


def matmul(left, right):
    return jnp.dot(left, right, preferred_element_type=jnp.float32)


def matmul_left_t(left, right):
    return lax.dot_general(
        left, right, (((0,), (0,)), ((), ())), preferred_element_type=jnp.float32
    )


def matmul_right_t(left, right):
    return lax.dot_general(
        left, right, (((1,), (1,)), ((), ())), preferred_element_type=jnp.float32
    )


def masked_scores(queries, keys, allowed):
    raw = jnp.einsum(
        "hqd,hkd->hqk", queries, keys, preferred_element_type=jnp.float32
    ) * HEAD_DIM ** (-0.5)
    return jnp.where(allowed[None], raw, -1e30)


def body(
    tokens,
    lengths,
    qkv_weight,
    query_bias,
    value_bias,
    out_weight,
    out_bias,
    norm_one_gain,
    norm_one_shift,
    ff_in_weight,
    ff_in_bias,
    ff_out_weight,
    ff_out_bias,
    norm_two_gain,
    norm_two_shift,
    out_grad,
):
    rows, width = tokens.shape
    heads = width // HEAD_DIM
    scale = HEAD_DIM ** (-0.5)
    devices = lax.axis_size("dp")
    if qkv_weight.shape[0] % 8 == 0:
        return whole_layer(
            tokens,
            lengths,
            (qkv_weight, out_weight, ff_in_weight, ff_out_weight),
            (
                query_bias,
                value_bias,
                out_bias,
                norm_one_gain,
                norm_one_shift,
                ff_out_bias,
                norm_two_gain,
                norm_two_shift,
                ff_in_bias,
            ),
            out_grad,
            devices,
        )
    (weight_qkv, weight_out, weight_in, weight_down), vectors = gather_params(
        (qkv_weight, out_weight, ff_in_weight, ff_out_weight),
        (
            query_bias,
            value_bias,
            out_bias,
            norm_one_gain,
            norm_one_shift,
            ff_out_bias,
            norm_two_gain,
            norm_two_shift,
            ff_in_bias,
        ),
        devices,
    )
    (bias_query, bias_value, bias_out, gain_first, shift_first, bias_down, gain_second,
     shift_second, bias_in) = vectors
    bounds = jnp.cumsum(lengths)
    position = jnp.arange(rows, dtype=jnp.int32)
    segments = jnp.sum((position[:, None] >= bounds[None, :]).astype(jnp.int32), axis=1)
    allowed = segments[:, None] == segments[None, :]
    zero_keys = jnp.zeros((width,), jnp.float32)
    qkv_bias = jnp.concatenate([as_float(bias_query), zero_keys, as_float(bias_value)])
    projected = to_low(matmul(tokens, weight_qkv) + qkv_bias)
    split = projected.reshape(rows, 3, heads, HEAD_DIM).transpose(1, 2, 0, 3)
    queries, keys, values = (split[0], split[1], split[2])
    scores = masked_scores(queries, keys, allowed)
    peak = jnp.max(scores, axis=-1, keepdims=True)
    log_total = peak + jnp.log(jnp.sum(jnp.exp(scores - peak), axis=-1, keepdims=True))
    attend = jnp.exp(scores - log_total)
    context = jnp.einsum("hqk,hkd->qhd", to_low(attend), values, preferred_element_type=jnp.float32)
    context = to_low(context.reshape(rows, width))
    first_sum = as_float(tokens) + matmul(context, weight_out) + as_float(bias_out)
    first_norm, norm_one_pull = jax.vjp(
        layer_norm, first_sum, as_float(gain_first), as_float(shift_first)
    )
    first_low = to_low(first_norm)
    pre_act = matmul(first_low, weight_in) + as_float(bias_in)
    activated = to_low(gelu_exact(pre_act))
    second_sum = first_norm + matmul(activated, weight_down) + as_float(bias_down)
    encoded, norm_two_pull = jax.vjp(
        layer_norm, second_sum, as_float(gain_second), as_float(shift_second)
    )
    grad_second, grad_gain_second, grad_shift_second = norm_two_pull(as_float(out_grad))
    grad_ff = to_low(grad_second)
    grad_weight_down = matmul_left_t(activated, grad_ff)
    grad_bias_down = jnp.sum(as_float(grad_ff), axis=0)
    grad_act = matmul_right_t(grad_ff, weight_down)
    gelu_pull = jax.vjp(gelu_exact, pre_act)[1]
    grad_pre = to_low(gelu_pull(grad_act)[0])
    grad_weight_in = matmul_left_t(first_low, grad_pre)
    grad_bias_in = jnp.sum(as_float(grad_pre), axis=0)
    grad_first = grad_second + matmul_right_t(grad_pre, weight_in)
    grad_first_sum, grad_gain_first, grad_shift_first = norm_one_pull(grad_first)
    grad_attn = to_low(grad_first_sum)
    grad_weight_out = matmul_left_t(context, grad_attn)
    grad_bias_out = jnp.sum(as_float(grad_attn), axis=0)
    grad_context = to_low(matmul_right_t(grad_attn, weight_out))
    grad_heads = grad_context.reshape(rows, heads, HEAD_DIM).transpose(1, 0, 2)
    again_scores = masked_scores(queries, keys, allowed)
    again_attend = jnp.exp(again_scores - log_total)
    grad_values = jnp.einsum(
        "hqk,hqd->hkd", to_low(again_attend), grad_heads, preferred_element_type=jnp.float32
    )
    grad_attend = jnp.einsum("hqd,hkd->hqk", grad_heads, values, preferred_element_type=jnp.float32)
    row_total = jnp.sum(grad_attend * again_attend, axis=-1, keepdims=True)
    grad_scores = to_low(again_attend * (grad_attend - row_total))
    grad_queries = (
        jnp.einsum("hqk,hkd->hqd", grad_scores, keys, preferred_element_type=jnp.float32) * scale
    )
    grad_keys = (
        jnp.einsum("hqk,hqd->hkd", grad_scores, queries, preferred_element_type=jnp.float32) * scale
    )
    grad_qkv = to_low(
        jnp.stack([grad_queries, grad_keys, grad_values])
        .transpose(2, 0, 1, 3)
        .reshape(rows, 3 * width)
    )
    grad_weight_qkv = matmul_left_t(tokens, grad_qkv)
    grad_columns = jnp.sum(as_float(grad_qkv), axis=0)
    grad_bias_query = grad_columns[:width]
    grad_bias_value = grad_columns[2 * width :]
    grad_tokens = grad_first_sum + matmul_right_t(grad_qkv, weight_qkv)
    (own_down, own_in, own_out, own_qkv), own = scatter_grads(
        (grad_weight_down, grad_weight_in, grad_weight_out, grad_weight_qkv),
        (
            grad_bias_query,
            grad_bias_value,
            grad_bias_out,
            grad_gain_first,
            grad_shift_first,
            grad_bias_down,
            grad_gain_second,
            grad_shift_second,
            grad_bias_in,
        ),
        devices,
    )
    return (
        to_low(encoded),
        grad_tokens,
        own_qkv,
        own[0],
        own[1],
        own_out,
        own[2],
        own[3],
        own[4],
        own_in,
        own[8],
        own_down,
        own[5],
        own[6],
        own[7],
    )


def solution(mesh):
    in_specs = (
        P("dp", None),
        P("dp"),
        P("dp", None),
        P("dp"),
        P("dp"),
        P("dp", None),
        P("dp"),
        P("dp"),
        P("dp"),
        P("dp", None),
        P("dp"),
        P("dp", None),
        P("dp"),
        P("dp"),
        P("dp"),
        P("dp", None),
    )
    out_specs = (
        P("dp", None),
        P("dp", None),
        P("dp", None),
        P("dp"),
        P("dp"),
        P("dp", None),
        P("dp"),
        P("dp"),
        P("dp"),
        P("dp", None),
        P("dp"),
        P("dp", None),
        P("dp"),
        P("dp"),
        P("dp"),
    )
    return jax.shard_map(body, mesh=mesh, in_specs=in_specs, out_specs=out_specs, check_vma=False)
```
